256 devices in a mesh: row: 32 (over y, z_hi, core), col: 8 (over x, z_lo).
Axes of the slice: x: 4, y: 4, z: 8 (z_hi: 4, z_lo: 2; z = z_hi * 2 + z_lo), core: 2. Of those that a mesh axis runs over, the one named last changes fastest.
Arguments:
- blocks: bfloat16 [65536, 4096], P('row', 'col'), may hold values from -0.046875 to 0.046875
- factors: float32 [128, 512, 512], P('row'), as said below
- block_live: int32 [128], P('row'), may hold values from 1 to 512, 49152 in all
Outputs:
- schur_matrix: float32 [4096, 4096], P('row', 'col')
- panel_factor: float32 [4096, 512], P('row', 'col')
The draws below stay inside these ranges and needn't reach their ends.
Inputs may be any that keep to these rules, and one draw needn't show every extreme that they name: `factors`: each block is lower triangular with a positive diagonal and zeros above it. `block_live`: rows of a block at or beyond its count are left out.
All inputs are finite; a program needn't handle non-finite values.
Results may differ from the reference program's by a relative error of at most 0.0014.
Values may be sent and summed in bfloat16 or wider, within the bound.
A program may use at most 128 MiB of HBM per device.

```python
import math
import jax
import jax.numpy as jnp
import numpy as np
from jax import lax

N = 4096
BLK = 512
LEAD = 512
BLOCKS = 128
P_SIZE = 65536


def draw_factors(key, part):
    first_key, second_key = jax.random.split(jax.random.fold_in(key, 17))
    strict = jax.random.normal(first_key, (BLOCKS, BLK, BLK), jnp.float32) * (0.5 / math.sqrt(BLK))
    strict = jnp.tril(strict, -1)
    diagonal = jax.random.uniform(second_key, (BLOCKS, BLK), jnp.float32, 1.0, 2.0)
    return strict + jnp.eye(BLK, dtype=jnp.float32)[None, :, :] * diagonal[:, :, None]


def strengthened(entries, rng, source, target, parts, factor):
    def block_of(axis_at):
        return (jnp.arange(entries.shape[axis_at]) // (entries.shape[axis_at] // parts)).reshape((-1,) + (1,) * (entries.ndim - 1 - axis_at))

    near = jax.random.permutation(rng, parts)[block_of(target)]
    far = (block_of(target) + parts // 2) % parts
    return jnp.where((block_of(source) == near) | (block_of(source) == far), factor * entries, entries)


def levels(own_key, extent, cuts, low, largest):
    def one(dim, blocks):
        draws = jax.random.uniform(jax.random.fold_in(jax.random.fold_in(own_key, 6), dim), (blocks,), jnp.float32, low / len(cuts), largest / len(cuts))
        return jnp.repeat(jnp.exp(draws), extent[dim] // blocks).reshape((-1,) + (1,) * (len(extent) - dim - 1))

    factor_of = one(*cuts[0])
    for cut in cuts[1:]:
        factor_of = factor_of * one(*cut)
    return factor_of


def split_up(number_of, total, reach, slope):
    loads = [(1 << 20) // math.isqrt(standing ** slope) + 1 for standing in range(2, number_of + 1)]
    rest, counts = total - reach - (number_of - 1), [1] * (number_of - 1)
    while rest > 0:
        movable = [i for i in range(number_of - 1) if counts[i] < reach]
        mass, remaining = sum([loads[i] for i in movable]), rest
        for i in movable:
            extra = min(reach - counts[i], max(1, remaining * loads[i] // mass), rest)
            counts[i] = counts[i] + extra
            rest = rest - extra
    return np.array([reach] + counts)


def ragged(own_key, number_of, total, reach, skew):
    if number_of == 2:
        one = jax.random.randint(own_key, (), max(1, total - reach), min(reach, total - 1) + 1)
        return jnp.stack([one, total - one])
    tallies = jnp.asarray(split_up(number_of, total, reach, skew), jnp.int32)
    pairs = (number_of - 1) // 2
    donor, taker = tallies[1:1 + 2 * pairs:2], tallies[2:2 + 2 * pairs:2]
    room = jnp.minimum(donor - 1, reach - taker)
    passed = jax.random.randint(jax.random.fold_in(own_key, 1), (pairs,), 0, 1 << 20) % (room + 1)
    tallies = tallies.at[1:1 + 2 * pairs:2].set(donor - passed).at[2:2 + 2 * pairs:2].set(taker + passed)
    return tallies[jax.random.permutation(jax.random.fold_in(own_key, 2), number_of)]


def bell_draw_with(key, extent, spread, bound, pieces, heavy, kind=jnp.bfloat16):
    drawn = spread * jax.random.normal(key, extent, jnp.float32)
    if pieces:
        drawn = drawn * levels(key, extent, pieces, -0.22, 0.18)
    return jnp.clip(strengthened(drawn, jax.random.fold_in(key, 3), *heavy), -bound, bound).astype(kind)


def setup_inputs(seed: int = 0) -> dict:
    streams_of = jax.random.split(jax.random.key(seed), 4)
    return {
        "blocks": bell_draw_with(streams_of[0], (P_SIZE, N), P_SIZE ** -0.5, 0.046875, ((0, 32), (1, 8)), (0, 1, 32, 2.75)),
        "factors": draw_factors(jax.random.fold_in(streams_of[3], 71), 0),
        "block_live": ragged(streams_of[2], BLOCKS, 3 * BLOCKS * BLK // 4, BLK, 1).astype(jnp.int32),
    }


def reference(blocks, factors, block_live):
    columns = blocks.shape[1]
    shaped = blocks.reshape(BLOCKS, BLK, columns)
    row_index = jnp.arange(BLK, dtype=jnp.int32)

    def accumulate(running, inputs):
        factor, segment, live_rows = inputs
        solved = jax.scipy.linalg.solve_triangular(factor, segment.astype(jnp.float32), lower=True)
        solved = jnp.where(row_index[:, None] < live_rows, solved, 0.0).astype(jnp.bfloat16)
        solved = lax.optimization_barrier(solved)
        widened = solved.astype(jnp.float32)
        return (running + jnp.dot(widened.T, widened, precision=lax.Precision.HIGHEST), None)
    schur_matrix, _ = lax.scan(accumulate, jnp.zeros((columns, columns), jnp.float32), (factors, shaped, block_live))
    leading_block = schur_matrix[:LEAD, :LEAD]
    lead_factor = jnp.linalg.cholesky(leading_block)
    lead_inverse = jax.scipy.linalg.solve_triangular(lead_factor, jnp.eye(LEAD, dtype=jnp.float32), lower=True)
    panel_factor = jnp.dot(schur_matrix[:, :LEAD], lead_inverse.T, precision=lax.Precision.HIGHEST)
    return (schur_matrix, panel_factor)
```

```python
import jax
import jax.numpy as jnp
from jax import lax
from jax.experimental import pallas as pl
from jax.experimental.pallas import tpu as pltpu
from jax.sharding import Mesh
from jax.sharding import PartitionSpec as P

HI = lax.Precision.HIGHEST


def dot_f32(a, b):
    return jnp.dot(a, b, precision=HI, preferred_element_type=jnp.float32)


def dot_bf16(a, b):
    return jnp.dot(a, b, preferred_element_type=jnp.float32)


def dot_lhs_t(a, b):
    return lax.dot_general(a, b, (((0,), (0,)), ((), ())), preferred_element_type=jnp.float32)


def three_parts(v):
    high = v.astype(jnp.bfloat16)
    rest = v - high.astype(jnp.float32)
    mid = rest.astype(jnp.bfloat16)
    return high, mid, (rest - mid.astype(jnp.float32)).astype(jnp.bfloat16)


def whiten_block(high, low, segment):
    top = dot_bf16(high[:256, :256], segment[:256]) + dot_bf16(low[:256, :256], segment[:256])
    bottom = dot_bf16(high[256:], segment) + dot_bf16(low[256:], segment)
    return top.astype(jnp.bfloat16), bottom.astype(jnp.bfloat16)


def prepare_kernel(live_ref, factors_ref, blocks_ref, high_ref, low_ref, own_ref, diag_ref,
                   packed, spread, small, wide, inverse):
    row = lax.broadcasted_iota(jnp.int32, (128, 128), 0)
    lane = lax.broadcasted_iota(jnp.int32, (128, 128), 1)
    same = (row // 16) == (lane // 16)
    for f in range(4):
        for d in range(4):
            tile = factors_ref[f, pl.ds(128 * d, 128), pl.ds(128 * d, 128)]
            tile = jnp.where(same, tile, 0.0)
            total = tile[0:16]
            for b in range(1, 8):
                total = total + tile[16 * b:16 * b + 16]
            packed[:, 4 * f + d, :] = total
    high, mid, low = three_parts(packed[...].reshape(256, 128))
    for j in range(16):
        pick = jnp.where(same & (row % 16 == j), 1.0, 0.0).astype(jnp.bfloat16)
        spread[j] = (dot_bf16(high, pick) + dot_bf16(mid, pick) + dot_bf16(low, pick)).reshape(16, 16, 128)
    lane16 = lax.broadcasted_iota(jnp.int32, (16, 128), 1) % 16
    rows = []
    for i in range(16):
        value = jnp.where(lane16 == i, 1.0, 0.0)
        for j in range(i):
            value = value - spread[j, i] * rows[j]
        value = value / spread[i, i]
        rows.append(value)
        small[i] = value
    row2 = lax.broadcasted_iota(jnp.int32, (256, 256), 0)
    lane2 = lax.broadcasted_iota(jnp.int32, (256, 256), 1)

    def grow(block, _):
        f, h = block // 2, block % 2
        tile = factors_ref[f, pl.ds(pl.multiple_of(256 * h, 256), 256), pl.ds(pl.multiple_of(256 * h, 256), 256)]
        for d in range(2):
            narrow = small[:, 2 * block + d, :]
            wide[pl.ds(128 * d, 128), :] = jnp.where(same, jnp.concatenate([narrow] * 8, axis=0), 0.0)
        zero = jnp.zeros((128, 128), jnp.float32)
        held = jnp.concatenate([
            jnp.concatenate([wide[0:128, :], zero], axis=1),
            jnp.concatenate([zero, wide[128:256, :]], axis=1)], axis=0)
        for s in (16, 32, 64, 128):
            mask = ((row2 // (2 * s)) == (lane2 // (2 * s))) & (row2 % (2 * s) >= s) & (lane2 % (2 * s) < s)
            cross = jnp.where(mask, tile, 0.0)
            lower = [slice(2 * s * g + s, 2 * s * g + 2 * s) for g in range(256 // (2 * s))]
            odd = lambda v: jnp.concatenate([v[sl] for sl in lower], axis=0)
            first = dot_f32(odd(cross), held)
            pieces = []
            for g in range(256 // (2 * s)):
                pieces.append(jnp.zeros((s, 256), jnp.float32))
                pieces.append(first[g * s:(g + 1) * s])
            second = dot_f32(odd(held), jnp.concatenate(pieces, axis=0))
            pieces = []
            for g in range(256 // (2 * s)):
                pieces.append(held[2 * s * g:2 * s * g + s])
                pieces.append(held[2 * s * g + s:2 * s * g + 2 * s] - second[g * s:(g + 1) * s])
            held = jnp.concatenate(pieces, axis=0)
        inverse[block] = held
        return _

    lax.fori_loop(0, 8, grow, 0)

    def finish(f, _):
        live = live_ref[f]
        first, last = inverse[2 * f], inverse[2 * f + 1]
        corner = -dot_f32(last, dot_f32(factors_ref[f, 256:512, 0:256], first))

        def put(value, r, c):
            index = lax.broadcasted_iota(jnp.int32, (256, 256), 0) + r
            value = jnp.where(index < live, value, 0.0)
            high = value.astype(jnp.bfloat16)
            high_ref[f, r:r + 256, c:c + 256] = high
            low_ref[f, r:r + 256, c:c + 256] = (value - high.astype(jnp.float32)).astype(jnp.bfloat16)

        put(first, 0, 0)
        put(corner, 256, 0)
        put(last, 256, 256)
        put(jnp.zeros((256, 256), jnp.float32), 0, 256)
        start = pl.multiple_of(512 * f, 512)
        top, bottom = whiten_block(high_ref[f], low_ref[f], blocks_ref[pl.ds(start, 512), :])
        own_ref[pl.ds(start, 256), :] = top
        own_ref[pl.ds(start + 256, 256), :] = bottom
        return _

    lax.fori_loop(0, 4, finish, 0)
    diag_ref[...] = dot_lhs_t(own_ref[...], own_ref[...])


def prepare(blocks, factors, live):
    vmem = pl.BlockSpec(memory_space=pltpu.VMEM)
    return pl.pallas_call(
        prepare_kernel,
        out_shape=(
            jax.ShapeDtypeStruct((4, 512, 512), jnp.bfloat16),
            jax.ShapeDtypeStruct((4, 512, 512), jnp.bfloat16),
            jax.ShapeDtypeStruct((2048, 512), jnp.bfloat16),
            jax.ShapeDtypeStruct((512, 512), jnp.float32),
        ),
        in_specs=[pl.BlockSpec(memory_space=pltpu.SMEM), vmem, vmem],
        out_specs=(vmem,) * 4,
        scratch_shapes=[
            pltpu.VMEM((16, 16, 128), jnp.float32),
            pltpu.VMEM((16, 16, 16, 128), jnp.float32),
            pltpu.VMEM((16, 16, 128), jnp.float32),
            pltpu.VMEM((256, 128), jnp.float32),
            pltpu.VMEM((8, 256, 256), jnp.float32),
        ],
        compiler_params=pltpu.CompilerParams(vmem_limit_bytes=48 << 20),
        cost_estimate=pl.CostEstimate(flops=16 << 30, bytes_accessed=14 << 20, transcendentals=0),
    )(live, factors, blocks)


def lead_kernel(lead_ref, out_ref, work, parts):
    work[...] = lead_ref[...]
    row = lax.broadcasted_iota(jnp.int32, (128, 128), 0)
    lane = lax.broadcasted_iota(jnp.int32, (128, 128), 1)
    sub = lax.broadcasted_iota(jnp.int32, (8, 128), 0)
    lan = lax.broadcasted_iota(jnp.int32, (8, 128), 1)

    def factor(p):
        base = 128 * p
        a = [work[base + 8 * g:base + 8 * g + 8, base:base + 128] for g in range(16)]
        x = [jnp.where(sub + 8 * g == lan, 1.0, 0.0) for g in range(16)]
        scale = []
        for k in range(128):
            g0, s0 = k // 8, k % 8
            arow = a[g0][s0:s0 + 1, :]
            xrow = x[g0][s0:s0 + 1, :]
            pivot = arow[:, k:k + 1]
            inv = 1.0 / pivot
            scale.append(pivot)
            arow_n = arow * inv
            xrow_n = xrow * inv
            for g in range(g0, 16):
                col = a[g][:, k:k + 1]
                if g == g0:
                    if s0 == 7:
                        continue
                    col = jnp.where(sub[:, :1] > s0, col, 0.0)
                if k < 127:
                    a[g] = a[g] - col * arow_n
                    x[g] = x[g] - col * xrow_n
        pivots = jnp.concatenate(scale, axis=0)
        whole = jnp.concatenate(x, axis=0)
        return whole * lax.rsqrt(pivots)

    for p in range(4):
        own = factor(p)
        parts[p] = own
        if p < 3:
            rest = 128 * (3 - p)
            base = 128 * p + 128
            below = work[base:512, base - 128:base]
            panel = lax.dot_general(below, own, (((1,), (1,)), ((), ())), precision=HI, preferred_element_type=jnp.float32)
            work[base:512, base - 128:base] = panel
            work[base:512, base:512] = work[base:512, base:512] - lax.dot_general(
                panel, panel, (((1,), (1,)), ((), ())), precision=HI, preferred_element_type=jnp.float32)
    zero = jnp.zeros((128, 128), jnp.float32)
    out_ref[0:256, 256:512] = jnp.zeros((256, 256), jnp.float32)
    for h in range(2):
        o = 256 * h
        first, last = parts[2 * h], parts[2 * h + 1]
        out_ref[o:o + 128, o:o + 128] = first
        out_ref[o:o + 128, o + 128:o + 256] = zero
        out_ref[o + 128:o + 256, o + 128:o + 256] = last
        out_ref[o + 128:o + 256, o:o + 128] = -dot_f32(last, dot_f32(work[o + 128:o + 256, o:o + 128], first))
    out_ref[256:512, 0:256] = -dot_f32(
        out_ref[256:512, 256:512], dot_f32(work[256:512, 0:256], out_ref[0:256, 0:256]))


def lead_inverse_of(lead):
    vmem = pl.BlockSpec(memory_space=pltpu.VMEM)
    return pl.pallas_call(
        lead_kernel,
        out_shape=jax.ShapeDtypeStruct((512, 512), jnp.float32),
        in_specs=[vmem],
        out_specs=vmem,
        scratch_shapes=[pltpu.VMEM((512, 512), jnp.float32), pltpu.VMEM((4, 128, 128), jnp.float32)],
        compiler_params=pltpu.CompilerParams(vmem_limit_bytes=24 << 20),
        cost_estimate=pl.CostEstimate(flops=40 << 30, bytes_accessed=2 << 20, transcendentals=0),
    )(lead)


AXES = ("y", "zh", "k", "x", "zl")
MESH = pl.DeviceIdType.MESH


def tiles_kernel(high_ref, low_ref, own_ref, near_ref, next_ref, far_ref, out_ref, pair, side, half):
    x, z = lax.axis_index("x"), lax.axis_index("zl")
    own_at, near_at = pl.multiple_of(512 * z, 512), pl.multiple_of(512 - 512 * z, 512)
    h = x // 2

    def whiten(f, _):
        start = pl.multiple_of(512 * f, 512)
        rows = pl.ds(start, 512)
        pair[rows, pl.ds(own_at, 512)] = own_ref[rows, :]
        high, low = high_ref[f], low_ref[f]
        top, bottom = whiten_block(high, low, near_ref[rows, :])
        pair[pl.ds(start, 256), pl.ds(near_at, 512)] = top
        pair[pl.ds(start + 256, 256), pl.ds(near_at, 512)] = bottom
        top, bottom = whiten_block(high, low, next_ref[rows, :])
        side[pl.ds(start, 256), :] = top
        side[pl.ds(start + 256, 256), :] = bottom
        return _

    lax.fori_loop(0, 4, whiten, 0)
    for f in range(2):
        top, bottom = whiten_block(high_ref[2 * h + f], low_ref[2 * h + f], far_ref[512 * f:512 * f + 512, :])
        half[512 * f:512 * f + 256, :] = top
        half[512 * f + 256:512 * f + 512, :] = bottom
    for p in range(2):
        for n in range(4):
            cols = slice(256 * n, 256 * n + 256)
            one = dot_lhs_t(side[:, 256 * p:256 * p + 256], pair[:, cols]).astype(jnp.bfloat16)
            two = dot_lhs_t(half[:, 256 * p:256 * p + 256], pair[pl.ds(pl.multiple_of(1024 * h, 1024), 1024), cols]).astype(jnp.bfloat16)
            for i in range(2):
                for j in range(2):
                    a, b = 2 * p + i, 2 * n + j
                    at = (1 - a % 2, 2 * (a // 2) + b % 2, b // 2)
                    out_ref[at[0], at[1], at[2], 0:128, :] = one[128 * i:128 * i + 128, 128 * j:128 * j + 128]
                    out_ref[at[0], at[1], at[2], 128:256, :] = two[128 * i:128 * i + 128, 128 * j:128 * j + 128]
    lhs = pair[:, pl.ds(pl.multiple_of(256 * z, 256), 256)]
    for n in range(2):
        zt = dot_lhs_t(lhs, pair[:, 512 + 256 * n:768 + 256 * n]).astype(jnp.bfloat16)
        for i in range(2):
            for j in range(2):
                b = 2 * n + j
                for s in range(4):
                    out_ref[1 - i, s, (b + 3) % 4, 256:288, :] = zt[128 * i + 32 * s:128 * i + 32 * s + 32, 128 * j:128 * j + 128]


def tiles(high, low, own, near, nxt, far):
    vmem = pl.BlockSpec(memory_space=pltpu.VMEM)
    return pl.pallas_call(
        tiles_kernel,
        out_shape=jax.ShapeDtypeStruct((2, 4, 4, 288, 128), jnp.bfloat16),
        in_specs=[vmem] * 6,
        out_specs=vmem,
        scratch_shapes=[
            pltpu.VMEM((2048, 1024), jnp.bfloat16),
            pltpu.VMEM((2048, 512), jnp.bfloat16),
            pltpu.VMEM((1024, 512), jnp.bfloat16),
        ],
        compiler_params=pltpu.CompilerParams(vmem_limit_bytes=48 << 20),
        cost_estimate=pl.CostEstimate(flops=14 << 30, bytes_accessed=14 << 20, transcendentals=0),
    )(high, low, own, near, nxt, far)


def remote(src, dst, send, recv, **where):
    return pltpu.make_async_remote_copy(
        src_ref=src, dst_ref=dst, send_sem=send, recv_sem=recv, device_id=where, device_id_type=MESH)


def wrapped(i):
    return lax.rem(i + 8, 4)


def greet(barrier, **where):
    pl.semaphore_signal(barrier, inc=1, device_id=where, device_id_type=MESH)


def row_partners(barrier, y, zh, k):
    greet(barrier, k=1 - k)
    for d in range(1, 4):
        greet(barrier, y=wrapped(y + d))
        greet(barrier, zh=wrapped(zh + d))


def lead_sum_kernel(in_ref, out_ref, from_k, part_k, from_y, part_y, from_zh, whole, send, recv):
    y, zh, k = lax.axis_index("y"), lax.axis_index("zh"), lax.axis_index("k")
    barrier = pltpu.get_barrier_semaphore()
    row_partners(barrier, y, zh, k)
    pl.semaphore_wait(barrier, 7)
    copy = remote(in_ref.at[1 - k], from_k, send.at[0], recv.at[0], k=1 - k)
    copy.start()
    copy.wait()
    part_k[...] = in_ref[k] + from_k[...]
    copies = []
    for d in range(1, 4):
        copy = remote(part_k.at[wrapped(y + d)], from_y.at[d - 1], send.at[d], recv.at[d], y=wrapped(y + d))
        copy.start()
        copies.append(copy)
    for copy in copies:
        copy.wait()
    part_y[...] = part_k[y] + from_y[0] + from_y[1] + from_y[2]
    copies = []
    for d in range(1, 4):
        copy = remote(part_y.at[wrapped(zh + d)], from_zh.at[d - 1], send.at[3 + d], recv.at[3 + d], zh=wrapped(zh + d))
        copy.start()
        copies.append(copy)
    for copy in copies:
        copy.wait()
    whole[k, y, zh] = part_y[zh] + from_zh[0] + from_zh[1] + from_zh[2]
    copies = []
    for d in range(1, 4):
        mine = whole.at[k, y, zh]
        copy = remote(mine, mine, send.at[6 + d], recv.at[6 + d], zh=wrapped(zh + d))
        copy.start()
        copies.append(copy)
    for copy in copies:
        copy.wait()
    copies = []
    for d in range(1, 4):
        mine = whole.at[k, y]
        copy = remote(mine, mine, send.at[9 + d], recv.at[9 + d], y=wrapped(y + d))
        copy.start()
        copies.append(copy)
    for copy in copies:
        copy.wait()
    copy = remote(whole.at[k], whole.at[k], send.at[13], recv.at[13], k=1 - k)
    copy.start()
    copy.wait()
    out_ref[...] = whole[...]


def lead_sum(diag):
    vmem = pl.BlockSpec(memory_space=pltpu.VMEM)
    f32 = jnp.float32
    return pl.pallas_call(
        lead_sum_kernel,
        out_shape=jax.ShapeDtypeStruct((2, 4, 4, 16, 512), f32),
        in_specs=[vmem],
        out_specs=vmem,
        scratch_shapes=[
            pltpu.VMEM((4, 4, 16, 512), f32),
            pltpu.VMEM((4, 4, 16, 512), f32),
            pltpu.VMEM((3, 4, 16, 512), f32),
            pltpu.VMEM((4, 16, 512), f32),
            pltpu.VMEM((3, 16, 512), f32),
            pltpu.VMEM((2, 4, 4, 16, 512), f32),
            pltpu.SemaphoreType.DMA((14,)),
            pltpu.SemaphoreType.DMA((14,)),
        ],
        compiler_params=pltpu.CompilerParams(
            vmem_limit_bytes=24 << 20, collective_id=0, has_side_effects=True),
        cost_estimate=pl.CostEstimate(flops=20 << 30, bytes_accessed=2 << 20, transcendentals=0),
    )(diag.reshape(2, 4, 4, 16, 512)).reshape(512, 512)


def spread_kernel(parts_ref, lead_ref, inverse_ref, out_ref, panel_ref,
                  from_k, part_k, from_y, part_y, from_zh, final, land, land_t, strips, strip_in,
                  send, recv, land_sem, land_t_sem, strip_sem, strip_send, panel_sem):
    y, zh, k = lax.axis_index("y"), lax.axis_index("zh"), lax.axis_index("k")
    x, z = lax.axis_index("x"), lax.axis_index("zl")
    f32 = jnp.float32
    leader = (x == 0) & (z == 0)
    zr, q = zh // 2, 2 * lax.rem(zh, 2) + k
    dx = wrapped(y - x)
    is_direct = (dx == 1) | (dx == 2)
    is_turned = (dx == 3) | (dx == 2)
    strip_direct = (dx == 0) & (zr == 0) & (z == 1)
    strip_turned = (dx == 0) & (zr == 1) & (z == 0)
    is_diag = (dx == 0) & (zr == z)

    barrier = pltpu.get_barrier_semaphore()
    row_partners(barrier, y, zh, k)

    @pl.when(is_direct)
    def _():
        for j in range(4):
            b = 4 * z + j
            greet(barrier, k=1 - lax.rem(q, 2), y=2 * (q // 2) + lax.rem(b, 2), zh=b // 2, x=x, zl=zr)

    @pl.when(is_turned)
    def _():
        for j in range(4):
            greet(barrier, k=1 - j % 2, y=2 * (j // 2) + k, zh=zh, x=y, zl=z)

    @pl.when(strip_direct)
    def _():
        for j in range(4):
            for s in range(4):
                greet(barrier, k=1 - k, y=s, zh=(j + 3) % 4, x=x, zl=zh)

    @pl.when(strip_turned)
    def _():
        for j in range(4):
            for s in range(4):
                greet(barrier, k=1 - j % 2, y=s, zh=lax.rem(2 * (zh - 2) + k + 3, 4), x=x, zl=j // 2)

    @pl.when(leader)
    def _():
        pl.semaphore_wait(barrier, 20)

    @pl.when(jnp.logical_not(leader))
    def _():
        greet(barrier, x=0, zl=0)
        pl.semaphore_wait(barrier, 13)

    copy = remote(parts_ref.at[1 - k], from_k, send.at[0], recv.at[0], k=1 - k)
    copy.start()
    copy.wait()
    for i in range(4):
        part_k[i] = (parts_ref[k, i].astype(f32) + from_k[i].astype(f32)).astype(jnp.bfloat16)
    copies = []
    for d in range(1, 4):
        copy = remote(part_k.at[wrapped(y + d)], from_y.at[d - 1], send.at[d], recv.at[d], y=wrapped(y + d))
        copy.start()
        copies.append(copy)
    for copy in copies:
        copy.wait()
    part_y[...] = ((part_k[y].astype(f32) + from_y[0].astype(f32)) + (from_y[1].astype(f32) + from_y[2].astype(f32))).astype(jnp.bfloat16)
    copies = []
    for d in range(1, 4):
        copy = remote(part_y.at[wrapped(zh + d)], from_zh.at[d - 1], send.at[3 + d], recv.at[3 + d], zh=wrapped(zh + d))
        copy.start()
        copies.append(copy)
    for copy in copies:
        copy.wait()
    final[...] = (part_y[zh].astype(f32) + from_zh[0].astype(f32)) + (from_zh[1].astype(f32) + from_zh[2].astype(f32))

    a, b = 2 * (y // 2) + 1 - k, 2 * zh + lax.rem(y, 2)
    a2, b2 = 1 - k, wrapped(zh + 1)
    one, two, strip = final.at[pl.ds(0, 128)], final.at[pl.ds(128, 128)], final.at[pl.ds(256, 32)]
    sent = [
        remote(one, land.at[lax.rem(b, 4)], send.at[7], land_sem.at[lax.rem(b, 4)],
               x=x, zl=b // 4, y=wrapped(x + 1), zh=2 * z + a // 2, k=lax.rem(a, 2)),
        remote(one, land.at[a], send.at[8], land_sem.at[a],
               x=wrapped(x + 1), zl=z, y=x, zh=b // 2, k=lax.rem(b, 2)),
        remote(two, land.at[lax.rem(b, 4)], send.at[9], land_sem.at[lax.rem(b, 4)],
               x=x, zl=b // 4, y=wrapped(x + 2), zh=2 * z + a // 2, k=lax.rem(a, 2)),
        remote(two, land_t.at[a], send.at[10], land_t_sem.at[a],
               x=wrapped(x + 2), zl=z, y=x, zh=b // 2, k=lax.rem(b, 2)),
        remote(strip, strips.at[b2, y], strip_send.at[0], strip_sem.at[4 * b2 + y],
               x=x, zl=1, y=x, zh=z, k=a2),
        remote(strip, strips.at[2 * z + a2, y], strip_send.at[1], strip_sem.at[4 * (2 * z + a2) + y],
               x=x, zl=0, y=x, zh=2 + b2 // 2, k=lax.rem(b2, 2)),
    ]
    for copy in sent:
        copy.start()

    def arrived(j):
        remote(one, land.at[j], send.at[7], land_sem.at[j], k=1 - k).wait_recv()

    def arrived_turned(j):
        remote(one, land_t.at[j], send.at[7], land_t_sem.at[j], k=1 - k).wait_recv()

    def arrived_strips(j):
        for s in range(4):
            remote(strip, strips.at[j, s], strip_send.at[0], strip_sem.at[4 * j + s], k=1 - k).wait_recv()
        return jnp.concatenate([strips[j, s] for s in range(4)], axis=0)

    @pl.when(is_diag)
    def _():
        out_ref[...] = lead_ref[pl.ds(pl.multiple_of(128 * q, 128), 128), :]

    @pl.when(dx == 1)
    def _():
        for j in range(4):
            arrived(j)
            out_ref[:, 128 * j:128 * j + 128] = land[j]

    @pl.when(dx == 3)
    def _():
        for j in range(4):
            arrived(j)
            out_ref[:, 128 * j:128 * j + 128] = land[j].T

    @pl.when(dx == 2)
    def _():
        for j in range(4):
            arrived(j)
            arrived_turned(j)
            out_ref[:, 128 * j:128 * j + 128] = land[j] + land_t[j].T

    @pl.when(strip_direct)
    def _():
        for j in range(4):
            out_ref[:, 128 * j:128 * j + 128] = arrived_strips(j)

    @pl.when(strip_turned)
    def _():
        for j in range(4):
            out_ref[:, 128 * j:128 * j + 128] = arrived_strips(j).T

    @pl.when(leader)
    def _():
        slab = out_ref[...]
        for c in range(8):
            strip_in[c] = lax.dot_general(
                slab, inverse_ref[64 * c:64 * c + 64, :], (((1,), (1,)), ((), ())), precision=HI, preferred_element_type=f32)
            if c:
                remote(strip_in.at[c], strip_in.at[0], panel_sem.at[c], panel_sem.at[0], x=c // 2, zl=c % 2).start()
        panel_ref[...] = strip_in[0]
        for c in range(1, 8):
            remote(strip_in.at[c], strip_in.at[0], panel_sem.at[c], panel_sem.at[0], x=c // 2, zl=c % 2).wait_send()

    @pl.when(jnp.logical_not(leader))
    def _():
        remote(strip_in.at[1], strip_in.at[0], panel_sem.at[1], panel_sem.at[0], k=1 - k).wait_recv()
        panel_ref[...] = strip_in[0]

    for copy in sent:
        copy.wait_send()


def spread(parts, lead, inverse):
    vmem = pl.BlockSpec(memory_space=pltpu.VMEM)
    f32, bf16 = jnp.float32, jnp.bfloat16
    dma = pltpu.SemaphoreType.DMA
    return pl.pallas_call(
        spread_kernel,
        out_shape=(jax.ShapeDtypeStruct((128, 512), f32), jax.ShapeDtypeStruct((128, 64), f32)),
        in_specs=[vmem] * 3,
        out_specs=(vmem, vmem),
        scratch_shapes=[
            pltpu.VMEM((4, 4, 288, 128), bf16),
            pltpu.VMEM((4, 4, 288, 128), bf16),
            pltpu.VMEM((3, 4, 288, 128), bf16),
            pltpu.VMEM((4, 288, 128), bf16),
            pltpu.VMEM((3, 288, 128), bf16),
            pltpu.VMEM((288, 128), f32),
            pltpu.VMEM((4, 128, 128), f32),
            pltpu.VMEM((4, 128, 128), f32),
            pltpu.VMEM((4, 4, 32, 128), f32),
            pltpu.VMEM((8, 128, 64), f32),
            dma((11,)), dma((7,)), dma((4,)), dma((4,)), dma((16,)), dma((2,)), dma((8,)),
        ],
        compiler_params=pltpu.CompilerParams(
            vmem_limit_bytes=32 << 20, collective_id=1, has_side_effects=True),
        cost_estimate=pl.CostEstimate(flops=20 << 30, bytes_accessed=4 << 20, transcendentals=0),
    )(parts, lead, inverse)


def shifted(value, axis, step, size):
    return lax.ppermute(value, axis, [(i, (i + step) % size) for i in range(size)])


def body(blocks, factors, block_live):
    x = lax.axis_index("x")
    outgoing = lax.dynamic_slice_in_dim(blocks, 1024 * (1 - x // 2), 1024, 0)
    far = shifted(shifted(outgoing, "x", 1, 4), "x", 1, 4)
    near = shifted(blocks, "zl", 1, 2)
    nxt = shifted(blocks, "x", -1, 4)
    high, low, own, diag = prepare(blocks, factors, block_live)
    lead = lead_sum(diag)
    inverse = lead_inverse_of(lead)
    near, nxt, far, inverse = lax.optimization_barrier((near, nxt, far, inverse))
    parts = tiles(high, low, own, near, nxt, far)
    return spread(parts, lead, inverse)


def solution(mesh):
    split = Mesh(mesh.devices.reshape(4, 4, 2, 4, 2), AXES)
    row, col = ("y", "zh", "k"), ("x", "zl")
    return jax.shard_map(
        body, mesh=split, in_specs=(P(row, col), P(row, None, None), P(row)),
        out_specs=(P(row, col), P(row, col)), check_vma=False)
```

```python
import jax
import jax.numpy as jnp
from jax import lax
from jax.experimental import pallas as pl
from jax.experimental.pallas import tpu as pltpu
from jax.sharding import Mesh
from jax.sharding import PartitionSpec as P

HI = lax.Precision.HIGHEST
STEP = 8
WAYS = 4


def dot_f32(a, b):
    return jnp.dot(a, b, precision=HI, preferred_element_type=jnp.float32)


def dot_bf16(a, b):
    return jnp.dot(a, b, preferred_element_type=jnp.float32)


def dot_lhs_t(a, b):
    return lax.dot_general(a, b, (((0,), (0,)), ((), ())), preferred_element_type=jnp.float32)


def three_parts(v):
    high = v.astype(jnp.bfloat16)
    rest = v - high.astype(jnp.float32)
    mid = rest.astype(jnp.bfloat16)
    return high, mid, (rest - mid.astype(jnp.float32)).astype(jnp.bfloat16)


def whiten_block(high, low, segment):
    top = dot_bf16(high[:256, :256], segment[:256]) + dot_bf16(low[:256, :256], segment[:256])
    bottom = dot_bf16(high[256:], segment) + dot_bf16(low[256:], segment)
    return top.astype(jnp.bfloat16), bottom.astype(jnp.bfloat16)


def packed_at(r, c):
    return pl.ds(128 * (r * (r + 1) // 2 + c), 128)


def prepare_kernel(live_ref, factors_ref, blocks_ref, high_ref, low_ref, own_ref, diag_ref,
                   packed, spread, small, wide, inverse):
    row = lax.broadcasted_iota(jnp.int32, (128, 128), 0)
    lane = lax.broadcasted_iota(jnp.int32, (128, 128), 1)
    same = (row // 16) == (lane // 16)
    for f in range(4):
        for d in range(4):
            tile = factors_ref[f, pl.ds(128 * d, 128), pl.ds(128 * d, 128)]
            tile = jnp.where(same, tile, 0.0)
            total = tile[0:16]
            for b in range(1, 8):
                total = total + tile[16 * b:16 * b + 16]
            packed[:, 4 * f + d, :] = total
    high, mid, low = three_parts(packed[...].reshape(256, 128))
    for j in range(16):
        pick = jnp.where(same & (row % 16 == j), 1.0, 0.0).astype(jnp.bfloat16)
        spread[j] = (dot_bf16(high, pick) + dot_bf16(mid, pick) + dot_bf16(low, pick)).reshape(16, 16, 128)
    lane16 = lax.broadcasted_iota(jnp.int32, (16, 128), 1) % 16
    rows = []
    for i in range(16):
        value = jnp.where(lane16 == i, 1.0, 0.0)
        for j in range(i):
            value = value - spread[j, i] * rows[j]
        value = value / spread[i, i]
        rows.append(value)
        small[i] = value
    row2 = lax.broadcasted_iota(jnp.int32, (256, 256), 0)
    lane2 = lax.broadcasted_iota(jnp.int32, (256, 256), 1)

    def spread_out(block, slot):
        for d in range(2):
            narrow = small[:, 2 * block + d, :]
            wide[slot, 128 * d:128 * d + 128, 128 * d:128 * d + 128] = jnp.where(
                same, jnp.concatenate([narrow] * 8, axis=0), 0.0)
            wide[slot, 128 * d:128 * d + 128, 128 - 128 * d:256 - 128 * d] = jnp.zeros((128, 128), jnp.float32)
        return wide[slot]

    def grow(group, _):
        blocks = [WAYS * group + w for w in range(WAYS)]
        at = [pl.ds(pl.multiple_of(256 * (b % 2), 256), 256) for b in blocks]
        held = [spread_out(b, w) for w, b in enumerate(blocks)]
        for s in (16, 32, 64, 128):
            mask = ((row2 // (2 * s)) == (lane2 // (2 * s))) & (row2 % (2 * s) >= s) & (lane2 % (2 * s) < s)
            lower = [slice(2 * s * g + s, 2 * s * g + 2 * s) for g in range(256 // (2 * s))]
            odd = lambda v: jnp.concatenate([v[sl] for sl in lower], axis=0)
            first = [dot_f32(odd(jnp.where(mask, factors_ref[b // 2, at[w], at[w]], 0.0)), held[w]) for w, b in enumerate(blocks)]
            full = []
            for w in range(WAYS):
                pieces = []
                for g in range(256 // (2 * s)):
                    pieces.append(jnp.zeros((s, 256), jnp.float32))
                    pieces.append(first[w][g * s:(g + 1) * s])
                full.append(jnp.concatenate(pieces, axis=0))
            second = [dot_f32(odd(held[w]), full[w]) for w in range(WAYS)]
            for w in range(WAYS):
                pieces = []
                for g in range(256 // (2 * s)):
                    pieces.append(held[w][2 * s * g:2 * s * g + s])
                    pieces.append(held[w][2 * s * g + s:2 * s * g + 2 * s] - second[w][g * s:(g + 1) * s])
                held[w] = jnp.concatenate(pieces, axis=0)
        for w, b in enumerate(blocks):
            inverse[b] = held[w]
        return _

    lax.fori_loop(0, 8 // WAYS, grow, 0)

    def finish(f, _):
        live = live_ref[f]
        first, last = inverse[2 * f], inverse[2 * f + 1]
        corner = -dot_f32(last, dot_f32(factors_ref[f, 256:512, 0:256], first))

        def put(value, r, c):
            index = lax.broadcasted_iota(jnp.int32, (256, 256), 0) + r
            value = jnp.where(index < live, value, 0.0)
            high = value.astype(jnp.bfloat16)
            high_ref[f, r:r + 256, c:c + 256] = high
            low_ref[f, r:r + 256, c:c + 256] = (value - high.astype(jnp.float32)).astype(jnp.bfloat16)

        put(first, 0, 0)
        put(corner, 256, 0)
        put(last, 256, 256)
        put(jnp.zeros((256, 256), jnp.float32), 0, 256)
        start = pl.multiple_of(512 * f, 512)
        top, bottom = whiten_block(high_ref[f], low_ref[f], blocks_ref[pl.ds(start, 512), :])
        own_ref[pl.ds(start, 256), :] = top
        own_ref[pl.ds(start + 256, 256), :] = bottom
        return _

    lax.fori_loop(0, 4, finish, 0)
    for big, small_col in ((0, 0), (1, 0), (1, 1)):
        tile = dot_lhs_t(own_ref[:, 256 * big:256 * big + 256], own_ref[:, 256 * small_col:256 * small_col + 256])
        for i in range(2):
            for j in range(2):
                r, c = 2 * big + i, 2 * small_col + j
                if r >= c:
                    diag_ref[packed_at(r, c), :] = tile[128 * i:128 * i + 128, 128 * j:128 * j + 128]


def prepare(blocks, factors, live):
    vmem = pl.BlockSpec(memory_space=pltpu.VMEM)
    return pl.pallas_call(
        prepare_kernel,
        out_shape=(
            jax.ShapeDtypeStruct((4, 512, 512), jnp.bfloat16),
            jax.ShapeDtypeStruct((4, 512, 512), jnp.bfloat16),
            jax.ShapeDtypeStruct((2048, 512), jnp.bfloat16),
            jax.ShapeDtypeStruct((1280, 128), jnp.float32),
        ),
        in_specs=[pl.BlockSpec(memory_space=pltpu.SMEM), vmem, vmem],
        out_specs=(vmem,) * 4,
        scratch_shapes=[
            pltpu.VMEM((16, 16, 128), jnp.float32),
            pltpu.VMEM((16, 16, 16, 128), jnp.float32),
            pltpu.VMEM((16, 16, 128), jnp.float32),
            pltpu.VMEM((WAYS, 256, 256), jnp.float32),
            pltpu.VMEM((8, 256, 256), jnp.float32),
        ],
        compiler_params=pltpu.CompilerParams(vmem_limit_bytes=48 << 20),
        cost_estimate=pl.CostEstimate(flops=16 << 30, bytes_accessed=14 << 20, transcendentals=0),
    )(live, factors, blocks)


def factor(work, p):
    sub = lax.broadcasted_iota(jnp.int32, (8, 128), 0)
    lan = lax.broadcasted_iota(jnp.int32, (8, 128), 1)
    base = 128 * p
    a = [work[base + 8 * g:base + 8 * g + 8, base:base + 128] for g in range(16)]
    x = [jnp.where(sub + 8 * g == lan, 1.0, 0.0) for g in range(16)]
    scale = []
    for k in range(0, 128, STEP):
        g0, s0 = k // 8, k % 8
        arow = [a[g0][s0 + j:s0 + j + 1, :] for j in range(STEP)]
        xrow = [x[g0][s0 + j:s0 + j + 1, :] for j in range(STEP)]
        cols = {g: [jnp.broadcast_to(a[g][:, k + j:k + j + 1], (8, 128)) for j in range(STEP)] for g in range(g0, 16)}
        entry = [[cols[g0][j][s0 + i:s0 + i + 1, :] for j in range(STEP)] for i in range(STEP)]
        ratio = [[None] * STEP for _ in range(STEP)]
        inv = []
        for j in range(STEP):
            inv.append(1.0 / entry[j][j])
            scale.append(entry[j][j])
            for i in range(j + 1, STEP):
                t = entry[i][j] * inv[j]
                ratio[i][j] = t
                for m in range(j + 1, i + 1):
                    entry[i][m] = entry[i][m] - t * entry[m][j]
                arow[i] = arow[i] - t * arow[j]
                xrow[i] = xrow[i] - t * xrow[j]
        arow_n = [arow[j] * inv[j] for j in range(STEP)]
        xrow_n = [xrow[j] * inv[j] for j in range(STEP)]
        for g in range(g0, 16):
            c = cols[g]
            for i in range(1, STEP):
                for j in range(i):
                    c[i] = c[i] - c[j] * ratio[i][j]
            if g == g0:
                c = [jnp.where(sub > s0 + j, c[j], 0.0) for j in range(STEP)]
                if s0 + STEP == 8 and STEP == 1:
                    continue
            for j in range(STEP):
                a[g] = a[g] - c[j] * arow_n[j]
                x[g] = x[g] - c[j] * xrow_n[j]
    whole = jnp.concatenate(x, axis=0)
    return whole * lax.rsqrt(jnp.concatenate(scale, axis=0))


def dot_rhs_t(a, b):
    return lax.dot_general(a, b, (((1,), (1,)), ((), ())), precision=HI, preferred_element_type=jnp.float32)


def eliminate(work, parts, p):
    own = factor(work, p)
    parts[p] = own
    if p < 3:
        base = 128 * p + 128
        panel = dot_rhs_t(work[base:512, base - 128:base], own)
        work[base:512, base - 128:base] = panel
        work[base:512, base:512] = work[base:512, base:512] - dot_rhs_t(panel, panel)


def assemble(work, parts, out_ref):
    zero = jnp.zeros((128, 128), jnp.float32)
    out_ref[0:256, 256:512] = jnp.zeros((256, 256), jnp.float32)
    for h in range(2):
        o = 256 * h
        first, last = parts[2 * h], parts[2 * h + 1]
        out_ref[o:o + 128, o:o + 128] = first
        out_ref[o:o + 128, o + 128:o + 256] = zero
        out_ref[o + 128:o + 256, o + 128:o + 256] = last
        out_ref[o + 128:o + 256, o:o + 128] = -dot_f32(last, dot_f32(work[o + 128:o + 256, o:o + 128], first))
    out_ref[256:512, 0:256] = -dot_f32(
        out_ref[256:512, 256:512], dot_f32(work[256:512, 0:256], out_ref[0:256, 0:256]))


AXES = ("y", "zh", "k", "x", "zl")
MESH = pl.DeviceIdType.MESH


def remote(src, dst, send, recv, **where):
    return pltpu.make_async_remote_copy(
        src_ref=src, dst_ref=dst, send_sem=send, recv_sem=recv, device_id=where, device_id_type=MESH)


def wrapped(i):
    return lax.rem(i + 8, 4)


def greet(barrier, **where):
    pl.semaphore_signal(barrier, inc=1, device_id=where, device_id_type=MESH)


def row_partners(barrier, y, zh, k):
    greet(barrier, k=1 - k)
    for d in range(1, 4):
        greet(barrier, y=wrapped(y + d))
        greet(barrier, zh=wrapped(zh + d))


def lead_sum_kernel(in_ref, out_ref, work, parts, from_k, part_k, from_y, part_y, from_zh, whole, send, recv):
    y, zh, k = lax.axis_index("y"), lax.axis_index("zh"), lax.axis_index("k")
    barrier = pltpu.get_barrier_semaphore()
    row_partners(barrier, y, zh, k)
    pl.semaphore_wait(barrier, 7)
    copy = remote(in_ref.at[1 - k], from_k, send.at[0], recv.at[0], k=1 - k)
    copy.start()
    copy.wait()
    part_k[...] = in_ref[k] + from_k[...]
    copies = []
    for d in range(1, 4):
        copy = remote(part_k.at[wrapped(y + d)], from_y.at[d - 1], send.at[d], recv.at[d], y=wrapped(y + d))
        copy.start()
        copies.append(copy)
    for copy in copies:
        copy.wait()
    part_y[...] = part_k[y] + from_y[0] + from_y[1] + from_y[2]
    copies = []
    for d in range(1, 4):
        copy = remote(part_y.at[wrapped(zh + d)], from_zh.at[d - 1], send.at[3 + d], recv.at[3 + d], zh=wrapped(zh + d))
        copy.start()
        copies.append(copy)
    for copy in copies:
        copy.wait()
    whole[k, y, zh] = part_y[zh] + from_zh[0] + from_zh[1] + from_zh[2]
    copies = []
    for d in range(1, 4):
        mine = whole.at[k, y, zh]
        copy = remote(mine, mine, send.at[6 + d], recv.at[6 + d], zh=wrapped(zh + d))
        copy.start()
        copies.append(copy)
    for copy in copies:
        copy.wait()
    copies = []
    for d in range(1, 4):
        mine = whole.at[k, y]
        copy = remote(mine, mine, send.at[9 + d], recv.at[9 + d], y=wrapped(y + d))
        copy.start()
        copies.append(copy)
    for copy in copies:
        copy.wait()
    copy = remote(whole.at[k], whole.at[k], send.at[13], recv.at[13], k=1 - k)
    copy.start()
    copy.wait()
    out_ref[...] = whole[...].reshape(1280, 128)
    for r in range(4):
        for c in range(r + 1):
            work[128 * r:128 * r + 128, 128 * c:128 * c + 128] = out_ref[packed_at(r, c), :]
            if r != c:
                work[128 * c:128 * c + 128, 128 * r:128 * r + 128] = jnp.zeros((128, 128), jnp.float32)
    eliminate(work, parts, 0)
    eliminate(work, parts, 1)


def lead_sum(diag):
    vmem = pl.BlockSpec(memory_space=pltpu.VMEM)
    f32 = jnp.float32
    return pl.pallas_call(
        lead_sum_kernel,
        out_shape=(
            jax.ShapeDtypeStruct((1280, 128), f32),
            jax.ShapeDtypeStruct((512, 512), f32),
            jax.ShapeDtypeStruct((2, 128, 128), f32),
        ),
        in_specs=[vmem],
        out_specs=(vmem,) * 3,
        scratch_shapes=[
            pltpu.VMEM((4, 4, 40, 128), f32),
            pltpu.VMEM((4, 4, 40, 128), f32),
            pltpu.VMEM((3, 4, 40, 128), f32),
            pltpu.VMEM((4, 40, 128), f32),
            pltpu.VMEM((3, 40, 128), f32),
            pltpu.VMEM((2, 4, 4, 40, 128), f32),
            pltpu.SemaphoreType.DMA((14,)),
            pltpu.SemaphoreType.DMA((14,)),
        ],
        compiler_params=pltpu.CompilerParams(
            vmem_limit_bytes=24 << 20, collective_id=0, has_side_effects=True),
        cost_estimate=pl.CostEstimate(flops=20 << 30, bytes_accessed=2 << 20, transcendentals=0),
    )(diag.reshape(2, 4, 4, 40, 128))


def finish_kernel(high_ref, low_ref, own_ref, near_ref, next_ref, far_ref, lead_ref, begun_ref, parts_ref,
                  out_ref, panel_ref, pair, side, half, tmp, work, parts, inverse,
                  mine_a, away_a, from_k_a, part_k_a, from_y_a, mine_y_a, part_y_a, from_zh_a,
                  mine_b, away_b, from_k_b, part_k_b, from_y_b, mine_y_b, part_y_b, from_zh_b,
                  final_a, final_b, land, land_t, strips, slab_out,
                  send, recv, last_send, land_sem, land_t_sem, strip_sem, strip_send, panel_sem):
    y, zh, k = lax.axis_index("y"), lax.axis_index("zh"), lax.axis_index("k")
    x, z = lax.axis_index("x"), lax.axis_index("zl")
    f32, bf16 = jnp.float32, jnp.bfloat16
    h = x // 2
    leader = (x == 0) & (z == 0)
    zr, q = zh // 2, 2 * lax.rem(zh, 2) + k
    dx = wrapped(y - x)
    is_direct = (dx == 1) | (dx == 2)
    is_turned = (dx == 3) | (dx == 2)
    strip_direct = (dx == 0) & (zr == 0) & (z == 1)
    strip_turned = (dx == 0) & (zr == 1) & (z == 0)
    is_diag = (dx == 0) & (zr == z)

    barrier = pltpu.get_barrier_semaphore()
    row_partners(barrier, y, zh, k)

    @pl.when(is_direct)
    def _():
        for j in range(4):
            b = 4 * z + j
            greet(barrier, k=1 - lax.rem(q, 2), y=2 * (q // 2) + lax.rem(b, 2), zh=b // 2, x=x, zl=zr)

    @pl.when(is_turned)
    def _():
        for j in range(4):
            greet(barrier, k=1 - j % 2, y=2 * (j // 2) + k, zh=zh, x=y, zl=z)

    @pl.when(strip_direct)
    def _():
        for j in range(4):
            for s in range(4):
                greet(barrier, k=1 - k, y=s, zh=(j + 3) % 4, x=x, zl=zh)

    @pl.when(strip_turned)
    def _():
        for j in range(4):
            for s in range(4):
                greet(barrier, k=1 - j % 2, y=s, zh=lax.rem(2 * (zh - 2) + k + 3, 4), x=x, zl=j // 2)

    own_at, near_at = pl.multiple_of(512 * z, 512), pl.multiple_of(512 - 512 * z, 512)

    def whiten(f, _):
        start = pl.multiple_of(512 * f, 512)
        rows = pl.ds(start, 512)
        pair[rows, pl.ds(own_at, 512)] = own_ref[rows, :]
        high, low = high_ref[f], low_ref[f]
        top, bottom = whiten_block(high, low, near_ref[rows, :])
        pair[pl.ds(start, 256), pl.ds(near_at, 512)] = top
        pair[pl.ds(start + 256, 256), pl.ds(near_at, 512)] = bottom
        top, bottom = whiten_block(high, low, next_ref[rows, :])
        side[pl.ds(start, 256), :] = top
        side[pl.ds(start + 256, 256), :] = bottom
        return _

    def place(value, slot, put):
        tmp[slot] = value.reshape(2, 128, 256)
        kept, gone = tmp[slot, 1 - k], tmp[slot, k].astype(bf16)
        for j in range(2):
            put(j, kept[:, 128 * j:128 * j + 128], gone[:, 128 * j:128 * j + 128])

    lax.fori_loop(0, 4, whiten, 0)
    for p in range(2):
        for n in range(4):
            def put(j, kept, gone):
                mine_a[2 * p + j, n, :, :] = kept
                away_a[2 * p + j, n, :, :] = gone
            place(dot_lhs_t(side[:, 256 * p:256 * p + 256], pair[:, 256 * n:256 * n + 256]), n % 2, put)

    @pl.when(leader)
    def _():
        pl.semaphore_wait(barrier, 20)

    @pl.when(jnp.logical_not(leader))
    def _():
        greet(barrier, x=0, zl=0)
        pl.semaphore_wait(barrier, 13)

    groups = (
        (0, 128, mine_a, away_a, from_k_a, part_k_a, from_y_a, mine_y_a, part_y_a, from_zh_a, final_a),
        (1, 160, mine_b, away_b, from_k_b, part_k_b, from_y_b, mine_y_b, part_y_b, from_zh_b, final_b),
    )

    def send_k(group):
        g, _, mine, away, from_k = group[:5]
        copy = remote(away, from_k, send.at[7 * g], recv.at[7 * g], k=1 - k)
        copy.start()
        return copy

    def send_y(group, copy):
        g, _, mine, away, from_k, part_k, from_y = group[:7]
        copy.wait()
        for i in range(4):
            total = mine[i] + from_k[i].astype(f32)
            mine[i] = total
            part_k[i] = total.astype(bf16)
        copies = []
        for d in range(1, 4):
            copies.append(remote(part_k.at[wrapped(y + d)], from_y.at[d - 1],
                                 send.at[7 * g + d], recv.at[7 * g + d], y=wrapped(y + d)))
            copies[-1].start()
        return copies

    def send_zh(group, copies):
        g, _, mine, away, from_k, part_k, from_y, mine_y, part_y, from_zh, final = group
        for copy in copies:
            copy.wait()
        total = (mine[y] + from_y[0].astype(f32)) + (from_y[1].astype(f32) + from_y[2].astype(f32))
        mine_y[...] = total
        part_y[...] = total.astype(bf16)
        copies = []
        for d in range(1, 4):
            copies.append(remote(part_y.at[wrapped(zh + d)], from_zh.at[d - 1],
                                 send.at[7 * g + 3 + d], recv.at[7 * g + 3 + d], zh=wrapped(zh + d)))
            copies[-1].start()
        return copies

    def end(group, copies):
        mine_y, part_y, from_zh, final = group[7:]
        for copy in copies:
            copy.wait()
        final[...] = (mine_y[zh] + from_zh[0].astype(f32)) + (from_zh[1].astype(f32) + from_zh[2].astype(f32))

    k_a = send_k(groups[0])
    for f in range(2):
        top, bottom = whiten_block(high_ref[2 * h + f], low_ref[2 * h + f], far_ref[512 * f:512 * f + 512, :])
        half[512 * f:512 * f + 256, :] = top
        half[512 * f + 256:512 * f + 512, :] = bottom
    for p in range(2):
        for n in range(4):
            def put(j, kept, gone):
                mine_b[2 * p + j, n, 0:128, :] = kept
                away_b[2 * p + j, n, 0:128, :] = gone
            place(dot_lhs_t(half[:, 256 * p:256 * p + 256],
                            pair[pl.ds(pl.multiple_of(1024 * h, 1024), 1024), 256 * n:256 * n + 256]), n % 2, put)
    for n in range(2):
        def put(j, kept, gone):
            for s in range(4):
                mine_b[s, (2 * n + j + 3) % 4, 128:160, :] = kept[32 * s:32 * s + 32]
                away_b[s, (2 * n + j + 3) % 4, 128:160, :] = gone[32 * s:32 * s + 32]
        place(dot_lhs_t(pair[:, pl.ds(pl.multiple_of(256 * z, 256), 256)],
                        pair[:, 512 + 256 * n:768 + 256 * n]), n % 2, put)
    k_b = send_k(groups[1])
    y_a = send_y(groups[0], k_a)
    work[...] = begun_ref[...]
    parts[0:2] = parts_ref[...]
    y_b = send_y(groups[1], k_b)
    eliminate(work, parts, 2)
    zh_a = send_zh(groups[0], y_a)
    eliminate(work, parts, 3)
    zh_b = send_zh(groups[1], y_b)
    end(groups[0], zh_a)

    a, b = 2 * (y // 2) + 1 - k, 2 * zh + lax.rem(y, 2)
    a2, b2 = 1 - k, wrapped(zh + 1)
    one, two, strip = final_a, final_b.at[pl.ds(0, 128)], final_b.at[pl.ds(128, 32)]
    sent = [
        remote(one, land.at[lax.rem(b, 4)], last_send.at[0], land_sem.at[lax.rem(b, 4)],
               x=x, zl=b // 4, y=wrapped(x + 1), zh=2 * z + a // 2, k=lax.rem(a, 2)),
        remote(one, land.at[a], last_send.at[1], land_sem.at[a],
               x=wrapped(x + 1), zl=z, y=x, zh=b // 2, k=lax.rem(b, 2)),
        remote(two, land.at[lax.rem(b, 4)], last_send.at[2], land_sem.at[lax.rem(b, 4)],
               x=x, zl=b // 4, y=wrapped(x + 2), zh=2 * z + a // 2, k=lax.rem(a, 2)),
        remote(two, land_t.at[a], last_send.at[3], land_t_sem.at[a],
               x=wrapped(x + 2), zl=z, y=x, zh=b // 2, k=lax.rem(b, 2)),
        remote(strip, strips.at[b2, y], strip_send.at[0], strip_sem.at[4 * b2 + y],
               x=x, zl=1, y=x, zh=z, k=a2),
        remote(strip, strips.at[2 * z + a2, y], strip_send.at[1], strip_sem.at[4 * (2 * z + a2) + y],
               x=x, zl=0, y=x, zh=2 + b2 // 2, k=lax.rem(b2, 2)),
    ]
    sent[0].start()
    sent[1].start()
    assemble(work, parts, inverse)
    end(groups[1], zh_b)
    for copy in sent[2:]:
        copy.start()

    def arrived(j):
        remote(one, land.at[j], last_send.at[0], land_sem.at[j], k=1 - k).wait_recv()

    def arrived_turned(j):
        remote(one, land_t.at[j], last_send.at[0], land_t_sem.at[j], k=1 - k).wait_recv()

    def arrived_strips(j):
        for s in range(4):
            remote(strip, strips.at[j, s], strip_send.at[0], strip_sem.at[4 * j + s], k=1 - k).wait_recv()
        return jnp.concatenate([strips[j, s] for s in range(4)], axis=0)

    @pl.when(is_diag)
    def _():
        for j in range(4):
            @pl.when(q >= j)
            def _():
                start = pl.multiple_of(128 * (q * (q + 1) // 2 + j), 128)
                out_ref[:, 128 * j:128 * j + 128] = lead_ref[pl.ds(start, 128), :]

            @pl.when(q < j)
            def _():
                start = pl.multiple_of(128 * (j * (j + 1) // 2 + q), 128)
                out_ref[:, 128 * j:128 * j + 128] = lead_ref[pl.ds(start, 128), :].T

    @pl.when(dx == 1)
    def _():
        for j in range(4):
            arrived(j)
            out_ref[:, 128 * j:128 * j + 128] = land[j]

    @pl.when(dx == 3)
    def _():
        for j in range(4):
            arrived(j)
            out_ref[:, 128 * j:128 * j + 128] = land[j].T

    @pl.when(dx == 2)
    def _():
        for j in range(4):
            arrived(j)
            arrived_turned(j)
            out_ref[:, 128 * j:128 * j + 128] = land[j] + land_t[j].T

    @pl.when(strip_direct)
    def _():
        for j in range(4):
            out_ref[:, 128 * j:128 * j + 128] = arrived_strips(j)

    @pl.when(strip_turned)
    def _():
        for j in range(4):
            out_ref[:, 128 * j:128 * j + 128] = arrived_strips(j).T

    @pl.when(leader)
    def _():
        slab = out_ref[...]
        for c in range(8):
            slab_out[c] = dot_rhs_t(slab, inverse[64 * c:64 * c + 64, :])
            if c:
                remote(slab_out.at[c], slab_out.at[0], panel_sem.at[c], panel_sem.at[0], x=c // 2, zl=c % 2).start()
        panel_ref[...] = slab_out[0]
        for c in range(1, 8):
            remote(slab_out.at[c], slab_out.at[0], panel_sem.at[c], panel_sem.at[0], x=c // 2, zl=c % 2).wait_send()

    @pl.when(jnp.logical_not(leader))
    def _():
        remote(slab_out.at[1], slab_out.at[0], panel_sem.at[1], panel_sem.at[0], k=1 - k).wait_recv()
        panel_ref[...] = slab_out[0]

    for copy in sent:
        copy.wait_send()


def finish(high, low, own, near, nxt, far, lead, begun, parts):
    vmem = pl.BlockSpec(memory_space=pltpu.VMEM)
    f32, bf16 = jnp.float32, jnp.bfloat16
    dma = pltpu.SemaphoreType.DMA

    def buffers(n):
        return [
            pltpu.VMEM((4, 4, n, 128), f32),
            pltpu.VMEM((4, 4, n, 128), bf16),
            pltpu.VMEM((4, 4, n, 128), bf16),
            pltpu.VMEM((4, 4, n, 128), bf16),
            pltpu.VMEM((3, 4, n, 128), bf16),
            pltpu.VMEM((4, n, 128), f32),
            pltpu.VMEM((4, n, 128), bf16),
            pltpu.VMEM((3, n, 128), bf16),
        ]

    return pl.pallas_call(
        finish_kernel,
        out_shape=(jax.ShapeDtypeStruct((128, 512), f32), jax.ShapeDtypeStruct((128, 64), f32)),
        in_specs=[vmem] * 9,
        out_specs=(vmem, vmem),
        scratch_shapes=[
            pltpu.VMEM((2048, 1024), bf16),
            pltpu.VMEM((2048, 512), bf16),
            pltpu.VMEM((1024, 512), bf16),
            pltpu.VMEM((2, 2, 128, 256), f32),
            pltpu.VMEM((512, 512), f32),
            pltpu.VMEM((4, 128, 128), f32),
            pltpu.VMEM((512, 512), f32),
            *buffers(128),
            *buffers(160),
            pltpu.VMEM((128, 128), f32),
            pltpu.VMEM((160, 128), f32),
            pltpu.VMEM((4, 128, 128), f32),
            pltpu.VMEM((4, 128, 128), f32),
            pltpu.VMEM((4, 4, 32, 128), f32),
            pltpu.VMEM((8, 128, 64), f32),
            dma((14,)), dma((14,)), dma((4,)), dma((4,)), dma((4,)), dma((16,)), dma((2,)), dma((8,)),
        ],
        compiler_params=pltpu.CompilerParams(
            vmem_limit_bytes=56 << 20, collective_id=1, has_side_effects=True),
        cost_estimate=pl.CostEstimate(flops=40 << 30, bytes_accessed=14 << 20, transcendentals=0),
    )(high, low, own, near, nxt, far, lead, begun, parts)


def shifted(value, axis, step, size):
    return lax.ppermute(value, axis, [(i, (i + step) % size) for i in range(size)])


def body(blocks, factors, block_live):
    x = lax.axis_index("x")
    outgoing = lax.dynamic_slice_in_dim(blocks, 1024 * (1 - x // 2), 1024, 0)
    far = shifted(shifted(outgoing, "x", 1, 4), "x", 1, 4)
    near = shifted(blocks, "zl", 1, 2)
    nxt = shifted(blocks, "x", -1, 4)
    high, low, own, diag = prepare(blocks, factors, block_live)
    lead, begun, parts = lead_sum(diag)
    return finish(high, low, own, near, nxt, far, lead, begun, parts)


def solution(mesh):
    split = Mesh(mesh.devices.reshape(4, 4, 2, 4, 2), AXES)
    row, col = ("y", "zh", "k"), ("x", "zl")
    return jax.shard_map(
        body, mesh=split, in_specs=(P(row, col), P(row, None, None), P(row)),
        out_specs=(P(row, col), P(row, col)), check_vma=False)
```

```python
import jax
import jax.numpy as jnp
from jax import lax
from jax.experimental import pallas as pl
from jax.experimental.pallas import tpu as pltpu
from jax.sharding import Mesh
from jax.sharding import PartitionSpec as P

HI = lax.Precision.HIGHEST
STEP = 8
WAYS = 4


def dot_f32(a, b):
    return jnp.dot(a, b, precision=HI, preferred_element_type=jnp.float32)


def dot_bf16(a, b):
    return jnp.dot(a, b, preferred_element_type=jnp.float32)


def dot_lhs_t(a, b):
    return lax.dot_general(a, b, (((0,), (0,)), ((), ())), preferred_element_type=jnp.float32)


def three_parts(v):
    high = v.astype(jnp.bfloat16)
    rest = v - high.astype(jnp.float32)
    mid = rest.astype(jnp.bfloat16)
    return high, mid, (rest - mid.astype(jnp.float32)).astype(jnp.bfloat16)


def whiten_block(high, low, segment):
    top = dot_bf16(high[:256, :256], segment[:256]) + dot_bf16(low[:256, :256], segment[:256])
    bottom = dot_bf16(high[256:], segment) + dot_bf16(low[256:], segment)
    return top.astype(jnp.bfloat16), bottom.astype(jnp.bfloat16)


def packed_at(r, c):
    return pl.ds(128 * (r * (r + 1) // 2 + c), 128)


def factor(work, p):
    sub = lax.broadcasted_iota(jnp.int32, (8, 128), 0)
    lan = lax.broadcasted_iota(jnp.int32, (8, 128), 1)
    base = 128 * p
    a = [work[base + 8 * g:base + 8 * g + 8, base:base + 128] for g in range(16)]
    x = [jnp.where(sub + 8 * g == lan, 1.0, 0.0) for g in range(16)]
    scale = []
    for k in range(0, 128, STEP):
        g0, s0 = k // 8, k % 8
        arow = [a[g0][s0 + j:s0 + j + 1, :] for j in range(STEP)]
        xrow = [x[g0][s0 + j:s0 + j + 1, :] for j in range(STEP)]
        cols = {g: [jnp.broadcast_to(a[g][:, k + j:k + j + 1], (8, 128)) for j in range(STEP)] for g in range(g0, 16)}
        entry = [[cols[g0][j][s0 + i:s0 + i + 1, :] for j in range(STEP)] for i in range(STEP)]
        ratio = [[None] * STEP for _ in range(STEP)]
        inv = []
        for j in range(STEP):
            inv.append(1.0 / entry[j][j])
            scale.append(entry[j][j])
            for i in range(j + 1, STEP):
                t = entry[i][j] * inv[j]
                ratio[i][j] = t
                for m in range(j + 1, i + 1):
                    entry[i][m] = entry[i][m] - t * entry[m][j]
                arow[i] = arow[i] - t * arow[j]
                xrow[i] = xrow[i] - t * xrow[j]
        arow_n = [arow[j] * inv[j] for j in range(STEP)]
        xrow_n = [xrow[j] * inv[j] for j in range(STEP)]
        for g in range(g0, 16):
            c = cols[g]
            for i in range(1, STEP):
                for j in range(i):
                    c[i] = c[i] - c[j] * ratio[i][j]
            if g == g0:
                c = [jnp.where(sub > s0 + j, c[j], 0.0) for j in range(STEP)]
                if s0 + STEP == 8 and STEP == 1:
                    continue
            for j in range(STEP):
                a[g] = a[g] - c[j] * arow_n[j]
                x[g] = x[g] - c[j] * xrow_n[j]
    whole = jnp.concatenate(x, axis=0)
    return whole * lax.rsqrt(jnp.concatenate(scale, axis=0))


def dot_rhs_t(a, b):
    return lax.dot_general(a, b, (((1,), (1,)), ((), ())), precision=HI, preferred_element_type=jnp.float32)


def eliminate(work, parts, p):
    own = factor(work, p)
    parts[p] = own
    if p < 3:
        base = 128 * p + 128
        panel = dot_rhs_t(work[base:512, base - 128:base], own)
        work[base:512, base - 128:base] = panel
        work[base:512, base:512] = work[base:512, base:512] - dot_rhs_t(panel, panel)


def assemble(work, parts, out_ref):
    zero = jnp.zeros((128, 128), jnp.float32)
    out_ref[0:256, 256:512] = jnp.zeros((256, 256), jnp.float32)
    for h in range(2):
        o = 256 * h
        first, last = parts[2 * h], parts[2 * h + 1]
        out_ref[o:o + 128, o:o + 128] = first
        out_ref[o:o + 128, o + 128:o + 256] = zero
        out_ref[o + 128:o + 256, o + 128:o + 256] = last
        out_ref[o + 128:o + 256, o:o + 128] = -dot_f32(last, dot_f32(work[o + 128:o + 256, o:o + 128], first))
    out_ref[256:512, 0:256] = -dot_f32(
        out_ref[256:512, 256:512], dot_f32(work[256:512, 0:256], out_ref[0:256, 0:256]))


AXES = ("y", "zh", "k", "x", "zl")
MESH = pl.DeviceIdType.MESH


def remote(src, dst, send, recv, **where):
    return pltpu.make_async_remote_copy(
        src_ref=src, dst_ref=dst, send_sem=send, recv_sem=recv, device_id=where, device_id_type=MESH)


def wrapped(i):
    return lax.rem(i + 8, 4)


def greet(barrier, **where):
    pl.semaphore_signal(barrier, inc=1, device_id=where, device_id_type=MESH)


def row_partners(barrier, y, zh, k):
    greet(barrier, k=1 - k)
    for d in range(1, 4):
        greet(barrier, y=wrapped(y + d))
        greet(barrier, zh=wrapped(zh + d))


def whole_kernel(live_ref, factors_ref, blocks_ref, out_ref, panel_ref,
                 packed, spread, small, wide, inverse_of, high_all, low_all,
                 near, nxt, relay, far, pair, side, half, acc, tmp,
                 lead_in, lead_from_k, lead_part_k, lead_from_y, lead_part_y, lead_from_zh, lead_ref,
                 work, parts, inverse,
                 mine_a, away_a, from_k_a, part_k_a, from_y_a, mine_y_a, part_y_a, from_zh_a,
                 mine_b, away_b, from_k_b, part_k_b, from_y_b, mine_y_b, part_y_b, from_zh_b,
                 final_a, final_b, land, land_t, strips, slab_out,
                 send, recv, last_send, land_sem, land_t_sem, strip_sem, strip_send, panel_sem,
                 gather_send, gather_recv, lead_send, lead_recv):
    y, zh, k = lax.axis_index("y"), lax.axis_index("zh"), lax.axis_index("k")
    x, z = lax.axis_index("x"), lax.axis_index("zl")
    f32, bf16 = jnp.float32, jnp.bfloat16
    h = x // 2
    leader = (x == 0) & (z == 0)
    zr, q = zh // 2, 2 * lax.rem(zh, 2) + k
    own_at, near_at = pl.multiple_of(512 * z, 512), pl.multiple_of(512 - 512 * z, 512)
    dx = wrapped(y - x)
    is_direct = (dx == 1) | (dx == 2)
    is_turned = (dx == 3) | (dx == 2)
    strip_direct = (dx == 0) & (zr == 0) & (z == 1)
    strip_turned = (dx == 0) & (zr == 1) & (z == 0)
    is_diag = (dx == 0) & (zr == z)

    barrier = pltpu.get_barrier_semaphore()
    row_partners(barrier, y, zh, k)

    @pl.when(is_direct)
    def _():
        for j in range(4):
            b = 4 * z + j
            greet(barrier, k=1 - lax.rem(q, 2), y=2 * (q // 2) + lax.rem(b, 2), zh=b // 2, x=x, zl=zr)

    @pl.when(is_turned)
    def _():
        for j in range(4):
            greet(barrier, k=1 - j % 2, y=2 * (j // 2) + k, zh=zh, x=y, zl=z)

    @pl.when(strip_direct)
    def _():
        for j in range(4):
            for s in range(4):
                greet(barrier, k=1 - k, y=s, zh=(j + 3) % 4, x=x, zl=zh)

    @pl.when(strip_turned)
    def _():
        for j in range(4):
            for s in range(4):
                greet(barrier, k=1 - j % 2, y=s, zh=lax.rem(2 * (zh - 2) + k + 3, 4), x=x, zl=j // 2)

    greet(barrier, zl=1 - z)
    greet(barrier, x=wrapped(x + 1))
    greet(barrier, x=wrapped(x - 1))

    @pl.when(leader)
    def _():
        pl.semaphore_wait(barrier, 23)

    @pl.when(jnp.logical_not(leader))
    def _():
        greet(barrier, x=0, zl=0)
        pl.semaphore_wait(barrier, 16)

    relayed, nears, nexts = [], [], []
    for f in range(4):
        rows = pl.ds(512 * f, 512)
        if f < 2:
            rows_far = pl.ds(pl.multiple_of(1024 * (1 - h) + 512 * f, 512), 512)
            relayed.append(remote(blocks_ref.at[rows_far], relay.at[f], gather_send.at[8 + f], gather_recv.at[8 + f], x=wrapped(x + 1)))
            relayed[f].start()
        nears.append(remote(blocks_ref.at[rows], near.at[f], gather_send.at[f], gather_recv.at[f], zl=1 - z))
        nears[f].start()
        nexts.append(remote(blocks_ref.at[rows], nxt.at[f], gather_send.at[4 + f], gather_recv.at[4 + f], x=wrapped(x - 1)))
        nexts[f].start()

    def prepare():
        row = lax.broadcasted_iota(jnp.int32, (128, 128), 0)
        lane = lax.broadcasted_iota(jnp.int32, (128, 128), 1)
        same = (row // 16) == (lane // 16)
        for f in range(4):
            for d in range(4):
                tile = factors_ref[f, pl.ds(128 * d, 128), pl.ds(128 * d, 128)]
                tile = jnp.where(same, tile, 0.0)
                total = tile[0:16]
                for b in range(1, 8):
                    total = total + tile[16 * b:16 * b + 16]
                packed[:, 4 * f + d, :] = total
        high, mid, low = three_parts(packed[...].reshape(256, 128))
        for j in range(16):
            pick = jnp.where(same & (row % 16 == j), 1.0, 0.0).astype(jnp.bfloat16)
            spread[j] = (dot_bf16(high, pick) + dot_bf16(mid, pick) + dot_bf16(low, pick)).reshape(16, 16, 128)
        lane16 = lax.broadcasted_iota(jnp.int32, (16, 128), 1) % 16
        rows = []
        for i in range(16):
            value = jnp.where(lane16 == i, 1.0, 0.0)
            for j in range(i):
                value = value - spread[j, i] * rows[j]
            value = value / spread[i, i]
            rows.append(value)
            small[i] = value
        row2 = lax.broadcasted_iota(jnp.int32, (256, 256), 0)
        lane2 = lax.broadcasted_iota(jnp.int32, (256, 256), 1)

        def spread_out(block, slot):
            for d in range(2):
                narrow = small[:, 2 * block + d, :]
                wide[slot, 128 * d:128 * d + 128, 128 * d:128 * d + 128] = jnp.where(
                    same, jnp.concatenate([narrow] * 8, axis=0), 0.0)
                wide[slot, 128 * d:128 * d + 128, 128 - 128 * d:256 - 128 * d] = jnp.zeros((128, 128), jnp.float32)
            return wide[slot]

        def grow(group, _):
            blocks = [WAYS * group + w for w in range(WAYS)]
            at = [pl.ds(pl.multiple_of(256 * (b % 2), 256), 256) for b in blocks]
            held = [spread_out(b, w) for w, b in enumerate(blocks)]
            for s in (16, 32, 64, 128):
                mask = ((row2 // (2 * s)) == (lane2 // (2 * s))) & (row2 % (2 * s) >= s) & (lane2 % (2 * s) < s)
                lower = [slice(2 * s * g + s, 2 * s * g + 2 * s) for g in range(256 // (2 * s))]
                odd = lambda v: jnp.concatenate([v[sl] for sl in lower], axis=0)
                first = [dot_f32(odd(jnp.where(mask, factors_ref[b // 2, at[w], at[w]], 0.0)), held[w]) for w, b in enumerate(blocks)]
                full = []
                for w in range(WAYS):
                    pieces = []
                    for g in range(256 // (2 * s)):
                        pieces.append(jnp.zeros((s, 256), jnp.float32))
                        pieces.append(first[w][g * s:(g + 1) * s])
                    full.append(jnp.concatenate(pieces, axis=0))
                second = [dot_f32(odd(held[w]), full[w]) for w in range(WAYS)]
                for w in range(WAYS):
                    pieces = []
                    for g in range(256 // (2 * s)):
                        pieces.append(held[w][2 * s * g:2 * s * g + s])
                        pieces.append(held[w][2 * s * g + s:2 * s * g + 2 * s] - second[w][g * s:(g + 1) * s])
                    held[w] = jnp.concatenate(pieces, axis=0)
            for w, b in enumerate(blocks):
                inverse_of[b] = held[w]
            return _

        lax.fori_loop(0, 8 // WAYS, grow, 0)

        def finish(f, _):
            live = live_ref[f]
            first, last = inverse_of[2 * f], inverse_of[2 * f + 1]
            corner = -dot_f32(last, dot_f32(factors_ref[f, 256:512, 0:256], first))

            def put(value, r, c):
                index = lax.broadcasted_iota(jnp.int32, (256, 256), 0) + r
                value = jnp.where(index < live, value, 0.0)
                high = value.astype(jnp.bfloat16)
                high_all[f, r:r + 256, c:c + 256] = high
                low_all[f, r:r + 256, c:c + 256] = (value - high.astype(jnp.float32)).astype(jnp.bfloat16)

            put(first, 0, 0)
            put(corner, 256, 0)
            put(last, 256, 256)
            put(jnp.zeros((256, 256), jnp.float32), 0, 256)
            start = pl.multiple_of(512 * f, 512)
            top, bottom = whiten_block(high_all[f], low_all[f], blocks_ref[pl.ds(start, 512), :])
            pair[pl.ds(start, 256), pl.ds(own_at, 512)] = top
            pair[pl.ds(start + 256, 256), pl.ds(own_at, 512)] = bottom
            return _

        lax.fori_loop(0, 4, finish, 0)
        for big, small_col in ((0, 0), (1, 0), (1, 1)):
            tile = dot_lhs_t(pair[:, pl.ds(pl.multiple_of(own_at + 256 * big, 256), 256)], pair[:, pl.ds(pl.multiple_of(own_at + 256 * small_col, 256), 256)])
            for i in range(2):
                for j in range(2):
                    r, c = 2 * big + i, 2 * small_col + j
                    if r >= c:
                        lead_in[packed_at(r, c), :] = tile[128 * i:128 * i + 128, 128 * j:128 * j + 128]

    def place(value, slot, put):
        tmp[slot] = value.reshape(2, 128, 256)
        kept, gone = tmp[slot, 1 - k], tmp[slot, k].astype(bf16)
        for j in range(2):
            put(j, kept[:, 128 * j:128 * j + 128], gone[:, 128 * j:128 * j + 128])

    groups = (
        (0, 128, mine_a, away_a, from_k_a, part_k_a, from_y_a, mine_y_a, part_y_a, from_zh_a, final_a),
        (1, 160, mine_b, away_b, from_k_b, part_k_b, from_y_b, mine_y_b, part_y_b, from_zh_b, final_b),
    )

    def send_k(group):
        g, _, mine, away, from_k = group[:5]
        copy = remote(away, from_k, send.at[7 * g], recv.at[7 * g], k=1 - k)
        copy.start()
        return copy

    def send_y(group, copy):
        g, _, mine, away, from_k, part_k, from_y = group[:7]
        copy.wait()
        for i in range(4):
            total = mine[i] + from_k[i].astype(f32)
            mine[i] = total
            part_k[i] = total.astype(bf16)
        copies = []
        for d in range(1, 4):
            copies.append(remote(part_k.at[wrapped(y + d)], from_y.at[d - 1],
                                 send.at[7 * g + d], recv.at[7 * g + d], y=wrapped(y + d)))
            copies[-1].start()
        return copies

    def send_zh(group, copies):
        g, _, mine, away, from_k, part_k, from_y, mine_y, part_y, from_zh, final = group
        for copy in copies:
            copy.wait()
        total = (mine[y] + from_y[0].astype(f32)) + (from_y[1].astype(f32) + from_y[2].astype(f32))
        mine_y[...] = total
        part_y[...] = total.astype(bf16)
        copies = []
        for d in range(1, 4):
            copies.append(remote(part_y.at[wrapped(zh + d)], from_zh.at[d - 1],
                                 send.at[7 * g + 3 + d], recv.at[7 * g + 3 + d], zh=wrapped(zh + d)))
            copies[-1].start()
        return copies

    def end(group, copies):
        mine_y, part_y, from_zh, final = group[7:]
        for copy in copies:
            copy.wait()
        final[...] = (mine_y[zh] + from_zh[0].astype(f32)) + (from_zh[1].astype(f32) + from_zh[2].astype(f32))

    def forward(f):
        relayed[f].wait()
        copy = remote(relay.at[f], far.at[f], gather_send.at[10 + f], gather_recv.at[10 + f], x=wrapped(x + 1))
        copy.start()
        return copy

    def land_chunk(f):
        nears[f].wait()
        nexts[f].wait()
        high, low = high_all[f], low_all[f]
        top, bottom = whiten_block(high, low, near[f])
        pair[512 * f:512 * f + 256, pl.ds(near_at, 512)] = top
        pair[512 * f + 256:512 * f + 512, pl.ds(near_at, 512)] = bottom
        top, bottom = whiten_block(high, low, nxt[f])
        side[0:256, :] = top
        side[256:512, :] = bottom
        for p in range(2):
            for n in range(4):
                value = dot_lhs_t(side[:, 256 * p:256 * p + 256], pair[512 * f:512 * f + 512, 256 * n:256 * n + 256])
                if f == 0:
                    acc[p, n] = value
                elif f < 3:
                    acc[p, n] += value
                else:
                    def put(j, kept, gone):
                        mine_a[2 * p + j, n, :, :] = kept
                        away_a[2 * p + j, n, :, :] = gone
                    place(acc[p, n] + value, n % 2, put)

    def lead_rows(ki, yi=None, zi=None):
        if yi is None:
            return pl.ds(pl.multiple_of(640 * ki, 8), 640)
        if zi is None:
            return pl.ds(pl.multiple_of(640 * ki + 160 * yi, 8), 160)
        return pl.ds(pl.multiple_of(640 * ki + 160 * yi + 40 * zi, 8), 40)

    def lead_k():
        copy = remote(lead_in.at[lead_rows(1 - k)], lead_from_k, lead_send.at[0], lead_recv.at[0], k=1 - k)
        copy.start()
        return copy

    def lead_y(copy):
        copy.wait()
        lead_part_k[...] = lead_in[lead_rows(k), :] + lead_from_k[...]
        copies = []
        for d in range(1, 4):
            copies.append(remote(lead_part_k.at[lead_rows(0, wrapped(y + d))], lead_from_y.at[d - 1],
                                 lead_send.at[d], lead_recv.at[d], y=wrapped(y + d)))
            copies[-1].start()
        return copies

    def lead_zh(copies):
        for copy in copies:
            copy.wait()
        lead_part_y[...] = lead_part_k[lead_rows(0, y), :] + lead_from_y[0] + lead_from_y[1] + lead_from_y[2]
        copies = []
        for d in range(1, 4):
            copies.append(remote(lead_part_y.at[lead_rows(0, 0, wrapped(zh + d))], lead_from_zh.at[d - 1],
                                 lead_send.at[3 + d], lead_recv.at[3 + d], zh=wrapped(zh + d)))
            copies[-1].start()
        return copies

    def lead_back_zh(copies):
        for copy in copies:
            copy.wait()
        rows = lead_rows(k, y, zh)
        lead_ref[rows, :] = (lead_part_y[lead_rows(0, 0, zh), :] + lead_from_zh[0] + lead_from_zh[1] + lead_from_zh[2])
        copies = []
        for d in range(1, 4):
            copies.append(remote(lead_ref.at[rows], lead_ref.at[rows], lead_send.at[6 + d], lead_recv.at[6 + d], zh=wrapped(zh + d)))
            copies[-1].start()
        return copies

    def lead_back_y(copies):
        for copy in copies:
            copy.wait()
        rows = lead_rows(k, y)
        copies = []
        for d in range(1, 4):
            copies.append(remote(lead_ref.at[rows], lead_ref.at[rows], lead_send.at[9 + d], lead_recv.at[9 + d], y=wrapped(y + d)))
            copies[-1].start()
        return copies

    def lead_back_k(copies):
        for copy in copies:
            copy.wait()
        rows = lead_rows(k)
        copy = remote(lead_ref.at[rows], lead_ref.at[rows], lead_send.at[13], lead_recv.at[13], k=1 - k)
        copy.start()
        return copy

    prepare()
    lead_step = lead_k()
    land_chunk(0)
    lead_step = lead_y(lead_step)
    fars = [forward(0)]
    land_chunk(1)
    fars.append(forward(1))
    lead_step = lead_zh(lead_step)
    lead_step = lead_back_zh(lead_step)
    land_chunk(2)
    lead_step = lead_back_y(lead_step)
    land_chunk(3)
    k_a = send_k(groups[0])
    lead_step = lead_back_k(lead_step)
    for f in range(2):
        fars[f].wait()
        top, bottom = whiten_block(high_all[2 * h + f], low_all[2 * h + f], far[f])
        half[512 * f:512 * f + 256, :] = top
        half[512 * f + 256:512 * f + 512, :] = bottom
    for p in range(2):
        for n in range(4):
            def put(j, kept, gone):
                mine_b[2 * p + j, n, 0:128, :] = kept
                away_b[2 * p + j, n, 0:128, :] = gone
            place(dot_lhs_t(half[:, 256 * p:256 * p + 256],
                            pair[pl.ds(pl.multiple_of(1024 * h, 1024), 1024), 256 * n:256 * n + 256]), n % 2, put)
    for n in range(2):
        def put(j, kept, gone):
            for s in range(4):
                mine_b[s, (2 * n + j + 3) % 4, 128:160, :] = kept[32 * s:32 * s + 32]
                away_b[s, (2 * n + j + 3) % 4, 128:160, :] = gone[32 * s:32 * s + 32]
        place(dot_lhs_t(pair[:, pl.ds(pl.multiple_of(256 * z, 256), 256)],
                        pair[:, 512 + 256 * n:768 + 256 * n]), n % 2, put)
    k_b = send_k(groups[1])
    y_a = send_y(groups[0], k_a)
    lead_step.wait()
    for r in range(4):
        for c in range(r + 1):
            work[128 * r:128 * r + 128, 128 * c:128 * c + 128] = lead_ref[packed_at(r, c), :]
            if r != c:
                work[128 * c:128 * c + 128, 128 * r:128 * r + 128] = jnp.zeros((128, 128), f32)
    y_b = send_y(groups[1], k_b)
    eliminate(work, parts, 0)
    eliminate(work, parts, 1)
    zh_a = send_zh(groups[0], y_a)
    eliminate(work, parts, 2)
    zh_b = send_zh(groups[1], y_b)
    eliminate(work, parts, 3)
    end(groups[0], zh_a)

    a, b = 2 * (y // 2) + 1 - k, 2 * zh + lax.rem(y, 2)
    a2, b2 = 1 - k, wrapped(zh + 1)
    one, two, strip = final_a, final_b.at[pl.ds(0, 128)], final_b.at[pl.ds(128, 32)]
    sent = [
        remote(one, land.at[lax.rem(b, 4)], last_send.at[0], land_sem.at[lax.rem(b, 4)],
               x=x, zl=b // 4, y=wrapped(x + 1), zh=2 * z + a // 2, k=lax.rem(a, 2)),
        remote(one, land.at[a], last_send.at[1], land_sem.at[a],
               x=wrapped(x + 1), zl=z, y=x, zh=b // 2, k=lax.rem(b, 2)),
        remote(two, land.at[lax.rem(b, 4)], last_send.at[2], land_sem.at[lax.rem(b, 4)],
               x=x, zl=b // 4, y=wrapped(x + 2), zh=2 * z + a // 2, k=lax.rem(a, 2)),
        remote(two, land_t.at[a], last_send.at[3], land_t_sem.at[a],
               x=wrapped(x + 2), zl=z, y=x, zh=b // 2, k=lax.rem(b, 2)),
        remote(strip, strips.at[b2, y], strip_send.at[0], strip_sem.at[4 * b2 + y],
               x=x, zl=1, y=x, zh=z, k=a2),
        remote(strip, strips.at[2 * z + a2, y], strip_send.at[1], strip_sem.at[4 * (2 * z + a2) + y],
               x=x, zl=0, y=x, zh=2 + b2 // 2, k=lax.rem(b2, 2)),
    ]
    sent[0].start()
    sent[1].start()
    assemble(work, parts, inverse)
    end(groups[1], zh_b)
    for copy in sent[2:]:
        copy.start()

    def arrived(j):
        remote(one, land.at[j], last_send.at[0], land_sem.at[j], k=1 - k).wait_recv()

    def arrived_turned(j):
        remote(one, land_t.at[j], last_send.at[0], land_t_sem.at[j], k=1 - k).wait_recv()

    def arrived_strips(j):
        for s in range(4):
            remote(strip, strips.at[j, s], strip_send.at[0], strip_sem.at[4 * j + s], k=1 - k).wait_recv()
        return jnp.concatenate([strips[j, s] for s in range(4)], axis=0)

    @pl.when(is_diag)
    def _():
        for j in range(4):
            @pl.when(q >= j)
            def _():
                start = pl.multiple_of(128 * (q * (q + 1) // 2 + j), 128)
                out_ref[:, 128 * j:128 * j + 128] = lead_ref[pl.ds(start, 128), :]

            @pl.when(q < j)
            def _():
                start = pl.multiple_of(128 * (j * (j + 1) // 2 + q), 128)
                out_ref[:, 128 * j:128 * j + 128] = lead_ref[pl.ds(start, 128), :].T

    @pl.when(dx == 1)
    def _():
        for j in range(4):
            arrived(j)
            out_ref[:, 128 * j:128 * j + 128] = land[j]

    @pl.when(dx == 3)
    def _():
        for j in range(4):
            arrived(j)
            out_ref[:, 128 * j:128 * j + 128] = land[j].T

    @pl.when(dx == 2)
    def _():
        for j in range(4):
            arrived(j)
            arrived_turned(j)
            out_ref[:, 128 * j:128 * j + 128] = land[j] + land_t[j].T

    @pl.when(strip_direct)
    def _():
        for j in range(4):
            out_ref[:, 128 * j:128 * j + 128] = arrived_strips(j)

    @pl.when(strip_turned)
    def _():
        for j in range(4):
            out_ref[:, 128 * j:128 * j + 128] = arrived_strips(j).T

    @pl.when(leader)
    def _():
        slab = out_ref[...]
        for c in range(8):
            slab_out[c] = dot_rhs_t(slab, inverse[64 * c:64 * c + 64, :])
            if c:
                remote(slab_out.at[c], slab_out.at[0], panel_sem.at[c], panel_sem.at[0], x=c // 2, zl=c % 2).start()
        panel_ref[...] = slab_out[0]
        for c in range(1, 8):
            remote(slab_out.at[c], slab_out.at[0], panel_sem.at[c], panel_sem.at[0], x=c // 2, zl=c % 2).wait_send()

    @pl.when(jnp.logical_not(leader))
    def _():
        remote(slab_out.at[1], slab_out.at[0], panel_sem.at[1], panel_sem.at[0], k=1 - k).wait_recv()
        panel_ref[...] = slab_out[0]

    for copy in sent:
        copy.wait_send()


def whole(blocks, factors, live):
    vmem = pl.BlockSpec(memory_space=pltpu.VMEM)
    f32, bf16 = jnp.float32, jnp.bfloat16
    dma = pltpu.SemaphoreType.DMA

    def buffers(n):
        return [
            pltpu.VMEM((4, 4, n, 128), f32),
            pltpu.VMEM((4, 4, n, 128), bf16),
            pltpu.VMEM((4, 4, n, 128), bf16),
            pltpu.VMEM((4, 4, n, 128), bf16),
            pltpu.VMEM((3, 4, n, 128), bf16),
            pltpu.VMEM((4, n, 128), f32),
            pltpu.VMEM((4, n, 128), bf16),
            pltpu.VMEM((3, n, 128), bf16),
        ]

    return pl.pallas_call(
        whole_kernel,
        out_shape=(jax.ShapeDtypeStruct((128, 512), f32), jax.ShapeDtypeStruct((128, 64), f32)),
        in_specs=[pl.BlockSpec(memory_space=pltpu.SMEM), vmem, vmem],
        out_specs=(vmem, vmem),
        scratch_shapes=[
            pltpu.VMEM((16, 16, 128), f32),
            pltpu.VMEM((16, 16, 16, 128), f32),
            pltpu.VMEM((16, 16, 128), f32),
            pltpu.VMEM((WAYS, 256, 256), f32),
            pltpu.VMEM((8, 256, 256), f32),
            pltpu.VMEM((4, 512, 512), bf16),
            pltpu.VMEM((4, 512, 512), bf16),
            pltpu.VMEM((4, 512, 512), bf16),
            pltpu.VMEM((4, 512, 512), bf16),
            pltpu.VMEM((2, 512, 512), bf16),
            pltpu.VMEM((2, 512, 512), bf16),
            pltpu.VMEM((2048, 1024), bf16),
            pltpu.VMEM((512, 512), bf16),
            pltpu.VMEM((1024, 512), bf16),
            pltpu.VMEM((2, 4, 256, 256), f32),
            pltpu.VMEM((2, 2, 128, 256), f32),
            pltpu.VMEM((1280, 128), f32),
            pltpu.VMEM((640, 128), f32),
            pltpu.VMEM((640, 128), f32),
            pltpu.VMEM((3, 160, 128), f32),
            pltpu.VMEM((160, 128), f32),
            pltpu.VMEM((3, 40, 128), f32),
            pltpu.VMEM((1280, 128), f32),
            pltpu.VMEM((512, 512), f32),
            pltpu.VMEM((4, 128, 128), f32),
            pltpu.VMEM((512, 512), f32),
            *buffers(128),
            *buffers(160),
            pltpu.VMEM((128, 128), f32),
            pltpu.VMEM((160, 128), f32),
            pltpu.VMEM((4, 128, 128), f32),
            pltpu.VMEM((4, 128, 128), f32),
            pltpu.VMEM((4, 4, 32, 128), f32),
            pltpu.VMEM((8, 128, 64), f32),
            dma((14,)), dma((14,)), dma((4,)), dma((4,)), dma((4,)), dma((16,)), dma((2,)), dma((8,)),
            dma((12,)), dma((12,)), dma((14,)), dma((14,)),
        ],
        compiler_params=pltpu.CompilerParams(
            vmem_limit_bytes=58 << 20, collective_id=0, has_side_effects=True),
        cost_estimate=pl.CostEstimate(flops=20 << 30, bytes_accessed=8 << 20, transcendentals=0),
    )(live, factors, blocks)


def body(blocks, factors, block_live):
    return whole(blocks, factors, block_live)


def solution(mesh):
    split = Mesh(mesh.devices.reshape(4, 4, 2, 4, 2), AXES)
    row, col = ("y", "zh", "k"), ("x", "zl")
    return jax.shard_map(
        body, mesh=split, in_specs=(P(row, col), P(row, None, None), P(row)),
        out_specs=(P(row, col), P(row, col)), check_vma=False)
```

```python
import jax
import jax.numpy as jnp
from jax import lax
from jax.experimental import pallas as pl
from jax.experimental.pallas import tpu as pltpu
from jax.sharding import Mesh
from jax.sharding import PartitionSpec as P

HI = lax.Precision.HIGHEST
STEP = 8
WAYS = 4


def dot_f32(a, b):
    return jnp.dot(a, b, precision=HI, preferred_element_type=jnp.float32)


def dot_bf16(a, b):
    return jnp.dot(a, b, preferred_element_type=jnp.float32)


def dot_lhs_t(a, b):
    return lax.dot_general(a, b, (((0,), (0,)), ((), ())), preferred_element_type=jnp.float32)


def three_parts(v):
    high = v.astype(jnp.bfloat16)
    rest = v - high.astype(jnp.float32)
    mid = rest.astype(jnp.bfloat16)
    return high, mid, (rest - mid.astype(jnp.float32)).astype(jnp.bfloat16)


def whiten_block(high, low, segment):
    top = dot_bf16(high[:256, :256], segment[:256]) + dot_bf16(low[:256, :256], segment[:256])
    bottom = dot_bf16(high[256:], segment) + dot_bf16(low[256:], segment)
    return top.astype(jnp.bfloat16), bottom.astype(jnp.bfloat16)


def packed_at(r, c):
    return pl.ds(128 * (r * (r + 1) // 2 + c), 128)


def factor(work, p):
    sub = lax.broadcasted_iota(jnp.int32, (8, 128), 0)
    lan = lax.broadcasted_iota(jnp.int32, (8, 128), 1)
    base = 128 * p
    a = [work[base + 8 * g:base + 8 * g + 8, base:base + 128] for g in range(16)]
    x = [jnp.where(sub + 8 * g == lan, 1.0, 0.0) for g in range(16)]
    scale = []
    for k in range(0, 128, STEP):
        g0, s0 = k // 8, k % 8
        arow = [a[g0][s0 + j:s0 + j + 1, :] for j in range(STEP)]
        xrow = [x[g0][s0 + j:s0 + j + 1, :] for j in range(STEP)]
        cols = {g: [jnp.broadcast_to(a[g][:, k + j:k + j + 1], (8, 128)) for j in range(STEP)] for g in range(g0, 16)}
        entry = [[cols[g0][j][s0 + i:s0 + i + 1, :] for j in range(STEP)] for i in range(STEP)]
        ratio = [[None] * STEP for _ in range(STEP)]
        inv = []
        for j in range(STEP):
            inv.append(1.0 / entry[j][j])
            scale.append(entry[j][j])
            for i in range(j + 1, STEP):
                t = entry[i][j] * inv[j]
                ratio[i][j] = t
                for m in range(j + 1, i + 1):
                    entry[i][m] = entry[i][m] - t * entry[m][j]
                arow[i] = arow[i] - t * arow[j]
                xrow[i] = xrow[i] - t * xrow[j]
        arow_n = [arow[j] * inv[j] for j in range(STEP)]
        xrow_n = [xrow[j] * inv[j] for j in range(STEP)]
        for g in range(g0, 16):
            c = cols[g]
            for i in range(1, STEP):
                for j in range(i):
                    c[i] = c[i] - c[j] * ratio[i][j]
            if g == g0:
                c = [jnp.where(sub > s0 + j, c[j], 0.0) for j in range(STEP)]
                if s0 + STEP == 8 and STEP == 1:
                    continue
            for j in range(STEP):
                a[g] = a[g] - c[j] * arow_n[j]
                x[g] = x[g] - c[j] * xrow_n[j]
    whole = jnp.concatenate(x, axis=0)
    return whole * lax.rsqrt(jnp.concatenate(scale, axis=0))


def dot_rhs_t(a, b):
    return lax.dot_general(a, b, (((1,), (1,)), ((), ())), precision=HI, preferred_element_type=jnp.float32)


def eliminate(work, parts, p):
    own = factor(work, p)
    parts[p] = own
    if p < 3:
        base = 128 * p + 128
        panel = dot_rhs_t(work[base:512, base - 128:base], own)
        work[base:512, base - 128:base] = panel
        work[base:512, base:512] = work[base:512, base:512] - dot_rhs_t(panel, panel)


def assemble(work, parts, out_ref):
    zero = jnp.zeros((128, 128), jnp.float32)
    out_ref[0:256, 256:512] = jnp.zeros((256, 256), jnp.float32)
    for h in range(2):
        o = 256 * h
        first, last = parts[2 * h], parts[2 * h + 1]
        out_ref[o:o + 128, o:o + 128] = first
        out_ref[o:o + 128, o + 128:o + 256] = zero
        out_ref[o + 128:o + 256, o + 128:o + 256] = last
        out_ref[o + 128:o + 256, o:o + 128] = -dot_f32(last, dot_f32(work[o + 128:o + 256, o:o + 128], first))
    out_ref[256:512, 0:256] = -dot_f32(
        out_ref[256:512, 256:512], dot_f32(work[256:512, 0:256], out_ref[0:256, 0:256]))


AXES = ("y", "zh", "k", "x", "zl")
MESH = pl.DeviceIdType.MESH


def remote(src, dst, send, recv, **where):
    return pltpu.make_async_remote_copy(
        src_ref=src, dst_ref=dst, send_sem=send, recv_sem=recv, device_id=where, device_id_type=MESH)


def wrapped(i):
    return lax.rem(i + 8, 4)


def greet(barrier, **where):
    pl.semaphore_signal(barrier, inc=1, device_id=where, device_id_type=MESH)


def row_partners(barrier, y, zh, k):
    greet(barrier, k=1 - k)
    for d in range(1, 4):
        greet(barrier, y=wrapped(y + d))
        greet(barrier, zh=wrapped(zh + d))


def whole_kernel(live_ref, factors_hbm, blocks_hbm, out_ref, panel_ref, factors_ref, blocks_ref, load_sem,
                 packed, spread, small, wide, inverse_of, high_all, low_all,
                 near, nxt, relay, far, pair, side, half, acc, tmp,
                 lead_in, lead_from_k, lead_part_k, lead_from_y, lead_part_y, lead_from_zh, lead_ref,
                 work, parts, inverse,
                 mine_a, away_a, from_k_a, part_k_a, from_y_a, mine_y_a, part_y_a, from_zh_a,
                 mine_b, away_b, from_k_b, part_k_b, from_y_b, mine_y_b, part_y_b, from_zh_b,
                 final_a, final_b, land, land_t, strips, slab_out,
                 send, recv, last_send, land_sem, land_t_sem, strip_sem, strip_send, panel_sem,
                 gather_send, gather_recv, lead_send, lead_recv):
    y, zh, k = lax.axis_index("y"), lax.axis_index("zh"), lax.axis_index("k")
    x, z = lax.axis_index("x"), lax.axis_index("zl")
    f32, bf16 = jnp.float32, jnp.bfloat16
    h = x // 2
    leader = (x == 0) & (z == 0)
    zr, q = zh // 2, 2 * lax.rem(zh, 2) + k
    own_at, near_at = pl.multiple_of(512 * z, 512), pl.multiple_of(512 - 512 * z, 512)
    dx = wrapped(y - x)
    is_direct = (dx == 1) | (dx == 2)
    is_turned = (dx == 3) | (dx == 2)
    strip_direct = (dx == 0) & (zr == 0) & (z == 1)
    strip_turned = (dx == 0) & (zr == 1) & (z == 0)
    is_diag = (dx == 0) & (zr == z)

    loads = [pltpu.make_async_copy(factors_hbm, factors_ref, load_sem.at[0]),
             pltpu.make_async_copy(blocks_hbm, blocks_ref, load_sem.at[1])]
    for copy in loads:
        copy.start()
    barrier = pltpu.get_barrier_semaphore()
    row_partners(barrier, y, zh, k)

    @pl.when(is_direct)
    def _():
        for j in range(4):
            b = 4 * z + j
            greet(barrier, k=1 - lax.rem(q, 2), y=2 * (q // 2) + lax.rem(b, 2), zh=b // 2, x=x, zl=zr)

    @pl.when(is_turned)
    def _():
        for j in range(4):
            greet(barrier, k=1 - j % 2, y=2 * (j // 2) + k, zh=zh, x=y, zl=z)

    @pl.when(strip_direct)
    def _():
        for j in range(4):
            for s in range(4):
                greet(barrier, k=1 - k, y=s, zh=(j + 3) % 4, x=x, zl=zh)

    @pl.when(strip_turned)
    def _():
        for j in range(4):
            for s in range(4):
                greet(barrier, k=1 - j % 2, y=s, zh=lax.rem(2 * (zh - 2) + k + 3, 4), x=x, zl=j // 2)

    greet(barrier, zl=1 - z)
    greet(barrier, x=wrapped(x + 1))
    greet(barrier, x=wrapped(x - 1))

    @pl.when(leader)
    def _():
        pl.semaphore_wait(barrier, 23)

    @pl.when(jnp.logical_not(leader))
    def _():
        greet(barrier, x=0, zl=0)
        pl.semaphore_wait(barrier, 16)

    relayed, nears, nexts = [], [], []
    for f in range(4):
        rows = pl.ds(512 * f, 512)
        if f < 2:
            rows_far = pl.ds(pl.multiple_of(1024 * (1 - h) + 512 * f, 512), 512)
            relayed.append(remote(blocks_hbm.at[rows_far], relay.at[f], gather_send.at[8 + f], gather_recv.at[8 + f], x=wrapped(x + 1)))
            relayed[f].start()
        nears.append(remote(blocks_hbm.at[rows], near.at[f], gather_send.at[f], gather_recv.at[f], zl=1 - z))
        nears[f].start()
        nexts.append(remote(blocks_hbm.at[rows], nxt.at[f], gather_send.at[4 + f], gather_recv.at[4 + f], x=wrapped(x - 1)))
        nexts[f].start()

    def prepare():
        row = lax.broadcasted_iota(jnp.int32, (128, 128), 0)
        lane = lax.broadcasted_iota(jnp.int32, (128, 128), 1)
        same = (row // 16) == (lane // 16)
        for f in range(4):
            for d in range(4):
                tile = factors_ref[f, pl.ds(128 * d, 128), pl.ds(128 * d, 128)]
                tile = jnp.where(same, tile, 0.0)
                total = tile[0:16]
                for b in range(1, 8):
                    total = total + tile[16 * b:16 * b + 16]
                packed[:, 4 * f + d, :] = total
        high, mid, low = three_parts(packed[...].reshape(256, 128))
        for j in range(16):
            pick = jnp.where(same & (row % 16 == j), 1.0, 0.0).astype(jnp.bfloat16)
            spread[j] = (dot_bf16(high, pick) + dot_bf16(mid, pick) + dot_bf16(low, pick)).reshape(16, 16, 128)
        lane16 = lax.broadcasted_iota(jnp.int32, (16, 128), 1) % 16
        rows = []
        for i in range(16):
            value = jnp.where(lane16 == i, 1.0, 0.0)
            for j in range(i):
                value = value - spread[j, i] * rows[j]
            value = value / spread[i, i]
            rows.append(value)
            small[i] = value
        row2 = lax.broadcasted_iota(jnp.int32, (256, 256), 0)
        lane2 = lax.broadcasted_iota(jnp.int32, (256, 256), 1)

        def spread_out(block, slot):
            for d in range(2):
                narrow = small[:, 2 * block + d, :]
                wide[slot, 128 * d:128 * d + 128, 128 * d:128 * d + 128] = jnp.where(
                    same, jnp.concatenate([narrow] * 8, axis=0), 0.0)
                wide[slot, 128 * d:128 * d + 128, 128 - 128 * d:256 - 128 * d] = jnp.zeros((128, 128), jnp.float32)
            return wide[slot]

        def grow(group, _):
            blocks = [WAYS * group + w for w in range(WAYS)]
            at = [pl.ds(pl.multiple_of(256 * (b % 2), 256), 256) for b in blocks]
            held = [spread_out(b, w) for w, b in enumerate(blocks)]
            for s in (16, 32, 64, 128):
                mask = ((row2 // (2 * s)) == (lane2 // (2 * s))) & (row2 % (2 * s) >= s) & (lane2 % (2 * s) < s)
                lower = [slice(2 * s * g + s, 2 * s * g + 2 * s) for g in range(256 // (2 * s))]
                odd = lambda v: jnp.concatenate([v[sl] for sl in lower], axis=0)
                first = [dot_f32(odd(jnp.where(mask, factors_ref[b // 2, at[w], at[w]], 0.0)), held[w]) for w, b in enumerate(blocks)]
                full = []
                for w in range(WAYS):
                    pieces = []
                    for g in range(256 // (2 * s)):
                        pieces.append(jnp.zeros((s, 256), jnp.float32))
                        pieces.append(first[w][g * s:(g + 1) * s])
                    full.append(jnp.concatenate(pieces, axis=0))
                second = [dot_f32(odd(held[w]), full[w]) for w in range(WAYS)]
                for w in range(WAYS):
                    pieces = []
                    for g in range(256 // (2 * s)):
                        pieces.append(held[w][2 * s * g:2 * s * g + s])
                        pieces.append(held[w][2 * s * g + s:2 * s * g + 2 * s] - second[w][g * s:(g + 1) * s])
                    held[w] = jnp.concatenate(pieces, axis=0)
            for w, b in enumerate(blocks):
                inverse_of[b] = held[w]
            return _

        lax.fori_loop(0, 8 // WAYS, grow, 0)

        def finish(f, _):
            live = live_ref[f]
            first, last = inverse_of[2 * f], inverse_of[2 * f + 1]
            corner = -dot_f32(last, dot_f32(factors_ref[f, 256:512, 0:256], first))

            def put(value, r, c):
                index = lax.broadcasted_iota(jnp.int32, (256, 256), 0) + r
                value = jnp.where(index < live, value, 0.0)
                high = value.astype(jnp.bfloat16)
                high_all[f, r:r + 256, c:c + 256] = high
                low_all[f, r:r + 256, c:c + 256] = (value - high.astype(jnp.float32)).astype(jnp.bfloat16)

            put(first, 0, 0)
            put(corner, 256, 0)
            put(last, 256, 256)
            put(jnp.zeros((256, 256), jnp.float32), 0, 256)
            start = pl.multiple_of(512 * f, 512)
            top, bottom = whiten_block(high_all[f], low_all[f], blocks_ref[pl.ds(start, 512), :])
            pair[pl.ds(start, 256), pl.ds(own_at, 512)] = top
            pair[pl.ds(start + 256, 256), pl.ds(own_at, 512)] = bottom
            return _

        lax.fori_loop(0, 4, finish, 0)
        for big, small_col in ((0, 0), (1, 0), (1, 1)):
            tile = dot_lhs_t(pair[:, pl.ds(pl.multiple_of(own_at + 256 * big, 256), 256)], pair[:, pl.ds(pl.multiple_of(own_at + 256 * small_col, 256), 256)])
            for i in range(2):
                for j in range(2):
                    r, c = 2 * big + i, 2 * small_col + j
                    if r >= c:
                        lead_in[packed_at(r, c), :] = tile[128 * i:128 * i + 128, 128 * j:128 * j + 128]

    def place(value, slot, put):
        tmp[slot] = value.reshape(2, 128, 256)
        kept, gone = tmp[slot, 1 - k], tmp[slot, k].astype(bf16)
        for j in range(2):
            put(j, kept[:, 128 * j:128 * j + 128], gone[:, 128 * j:128 * j + 128])

    groups = (
        (0, 128, mine_a, away_a, from_k_a, part_k_a, from_y_a, mine_y_a, part_y_a, from_zh_a, final_a),
        (1, 160, mine_b, away_b, from_k_b, part_k_b, from_y_b, mine_y_b, part_y_b, from_zh_b, final_b),
    )

    def send_k(group):
        g, _, mine, away, from_k = group[:5]
        copy = remote(away, from_k, send.at[7 * g], recv.at[7 * g], k=1 - k)
        copy.start()
        return copy

    def send_y(group, copy):
        g, _, mine, away, from_k, part_k, from_y = group[:7]
        copy.wait()
        for i in range(4):
            total = mine[i] + from_k[i].astype(f32)
            mine[i] = total
            part_k[i] = total.astype(bf16)
        copies = []
        for d in range(1, 4):
            copies.append(remote(part_k.at[wrapped(y + d)], from_y.at[d - 1],
                                 send.at[7 * g + d], recv.at[7 * g + d], y=wrapped(y + d)))
            copies[-1].start()
        return copies

    def send_zh(group, copies):
        g, _, mine, away, from_k, part_k, from_y, mine_y, part_y, from_zh, final = group
        for copy in copies:
            copy.wait()
        total = (mine[y] + from_y[0].astype(f32)) + (from_y[1].astype(f32) + from_y[2].astype(f32))
        mine_y[...] = total
        part_y[...] = total.astype(bf16)
        copies = []
        for d in range(1, 4):
            copies.append(remote(part_y.at[wrapped(zh + d)], from_zh.at[d - 1],
                                 send.at[7 * g + 3 + d], recv.at[7 * g + 3 + d], zh=wrapped(zh + d)))
            copies[-1].start()
        return copies

    def end(group, copies):
        mine_y, part_y, from_zh, final = group[7:]
        for copy in copies:
            copy.wait()
        final[...] = (mine_y[zh] + from_zh[0].astype(f32)) + (from_zh[1].astype(f32) + from_zh[2].astype(f32))

    def forward(f):
        relayed[f].wait()
        copy = remote(relay.at[f], far.at[f], gather_send.at[10 + f], gather_recv.at[10 + f], x=wrapped(x + 1))
        copy.start()
        return copy

    def land_chunk(f):
        nears[f].wait()
        nexts[f].wait()
        high, low = high_all[f], low_all[f]
        top, bottom = whiten_block(high, low, near[f])
        pair[512 * f:512 * f + 256, pl.ds(near_at, 512)] = top
        pair[512 * f + 256:512 * f + 512, pl.ds(near_at, 512)] = bottom
        top, bottom = whiten_block(high, low, nxt[f])
        side[0:256, :] = top
        side[256:512, :] = bottom
        for p in range(2):
            for n in range(4):
                value = dot_lhs_t(side[:, 256 * p:256 * p + 256], pair[512 * f:512 * f + 512, 256 * n:256 * n + 256])
                if f == 0:
                    acc[p, n] = value
                elif f < 3:
                    acc[p, n] += value
                else:
                    def put(j, kept, gone):
                        mine_a[2 * p + j, n, :, :] = kept
                        away_a[2 * p + j, n, :, :] = gone
                    place(acc[p, n] + value, n % 2, put)

    def lead_rows(ki, yi=None, zi=None):
        if yi is None:
            return pl.ds(pl.multiple_of(640 * ki, 8), 640)
        if zi is None:
            return pl.ds(pl.multiple_of(640 * ki + 160 * yi, 8), 160)
        return pl.ds(pl.multiple_of(640 * ki + 160 * yi + 40 * zi, 8), 40)

    def lead_k():
        copy = remote(lead_in.at[lead_rows(1 - k)], lead_from_k, lead_send.at[0], lead_recv.at[0], k=1 - k)
        copy.start()
        return copy

    def lead_y(copy):
        copy.wait()
        lead_part_k[...] = lead_in[lead_rows(k), :] + lead_from_k[...]
        copies = []
        for d in range(1, 4):
            copies.append(remote(lead_part_k.at[lead_rows(0, wrapped(y + d))], lead_from_y.at[d - 1],
                                 lead_send.at[d], lead_recv.at[d], y=wrapped(y + d)))
            copies[-1].start()
        return copies

    def lead_zh(copies):
        for copy in copies:
            copy.wait()
        lead_part_y[...] = lead_part_k[lead_rows(0, y), :] + lead_from_y[0] + lead_from_y[1] + lead_from_y[2]
        copies = []
        for d in range(1, 4):
            copies.append(remote(lead_part_y.at[lead_rows(0, 0, wrapped(zh + d))], lead_from_zh.at[d - 1],
                                 lead_send.at[3 + d], lead_recv.at[3 + d], zh=wrapped(zh + d)))
            copies[-1].start()
        return copies

    def lead_back_zh(copies):
        for copy in copies:
            copy.wait()
        rows = lead_rows(k, y, zh)
        lead_ref[rows, :] = (lead_part_y[lead_rows(0, 0, zh), :] + lead_from_zh[0] + lead_from_zh[1] + lead_from_zh[2])
        copies = []
        for d in range(1, 4):
            copies.append(remote(lead_ref.at[rows], lead_ref.at[rows], lead_send.at[6 + d], lead_recv.at[6 + d], zh=wrapped(zh + d)))
            copies[-1].start()
        return copies

    def lead_back_y(copies):
        for copy in copies:
            copy.wait()
        rows = lead_rows(k, y)
        copies = []
        for d in range(1, 4):
            copies.append(remote(lead_ref.at[rows], lead_ref.at[rows], lead_send.at[9 + d], lead_recv.at[9 + d], y=wrapped(y + d)))
            copies[-1].start()
        return copies

    def lead_back_k(copies):
        for copy in copies:
            copy.wait()
        rows = lead_rows(k)
        copy = remote(lead_ref.at[rows], lead_ref.at[rows], lead_send.at[13], lead_recv.at[13], k=1 - k)
        copy.start()
        return copy

    for copy in loads:
        copy.wait()
    prepare()
    fars = [forward(0)]
    lead_step = lead_k()
    land_chunk(0)
    lead_step = lead_y(lead_step)
    fars.append(forward(1))
    land_chunk(1)
    lead_step = lead_zh(lead_step)
    land_chunk(2)
    land_chunk(3)
    k_a = send_k(groups[0])
    lead_step = lead_back_zh(lead_step)
    for f in range(2):
        fars[f].wait()
        top, bottom = whiten_block(high_all[2 * h + f], low_all[2 * h + f], far[f])
        half[512 * f:512 * f + 256, :] = top
        half[512 * f + 256:512 * f + 512, :] = bottom
    y_a = send_y(groups[0], k_a)
    for p in range(2):
        for n in range(4):
            def put(j, kept, gone):
                mine_b[2 * p + j, n, 0:128, :] = kept
                away_b[2 * p + j, n, 0:128, :] = gone
            place(dot_lhs_t(half[:, 256 * p:256 * p + 256],
                            pair[pl.ds(pl.multiple_of(1024 * h, 1024), 1024), 256 * n:256 * n + 256]), n % 2, put)
    for n in range(2):
        def put(j, kept, gone):
            for s in range(4):
                mine_b[s, (2 * n + j + 3) % 4, 128:160, :] = kept[32 * s:32 * s + 32]
                away_b[s, (2 * n + j + 3) % 4, 128:160, :] = gone[32 * s:32 * s + 32]
        place(dot_lhs_t(pair[:, pl.ds(pl.multiple_of(256 * z, 256), 256)],
                        pair[:, 512 + 256 * n:768 + 256 * n]), n % 2, put)
    k_b = send_k(groups[1])
    lead_step = lead_back_y(lead_step)
    y_b = send_y(groups[1], k_b)
    zh_a = send_zh(groups[0], y_a)
    lead_step = lead_back_k(lead_step)
    lead_step.wait()
    for r in range(4):
        for c in range(r + 1):
            work[128 * r:128 * r + 128, 128 * c:128 * c + 128] = lead_ref[packed_at(r, c), :]
            if r != c:
                work[128 * c:128 * c + 128, 128 * r:128 * r + 128] = jnp.zeros((128, 128), f32)
    eliminate(work, parts, 0)
    zh_b = send_zh(groups[1], y_b)
    end(groups[0], zh_a)

    a, b = 2 * (y // 2) + 1 - k, 2 * zh + lax.rem(y, 2)
    a2, b2 = 1 - k, wrapped(zh + 1)
    one, two, strip = final_a, final_b.at[pl.ds(0, 128)], final_b.at[pl.ds(128, 32)]
    sent = [
        remote(one, land.at[lax.rem(b, 4)], last_send.at[0], land_sem.at[lax.rem(b, 4)],
               x=x, zl=b // 4, y=wrapped(x + 1), zh=2 * z + a // 2, k=lax.rem(a, 2)),
        remote(one, land.at[a], last_send.at[1], land_sem.at[a],
               x=wrapped(x + 1), zl=z, y=x, zh=b // 2, k=lax.rem(b, 2)),
        remote(two, land.at[lax.rem(b, 4)], last_send.at[2], land_sem.at[lax.rem(b, 4)],
               x=x, zl=b // 4, y=wrapped(x + 2), zh=2 * z + a // 2, k=lax.rem(a, 2)),
        remote(two, land_t.at[a], last_send.at[3], land_t_sem.at[a],
               x=wrapped(x + 2), zl=z, y=x, zh=b // 2, k=lax.rem(b, 2)),
        remote(strip, strips.at[b2, y], strip_send.at[0], strip_sem.at[4 * b2 + y],
               x=x, zl=1, y=x, zh=z, k=a2),
        remote(strip, strips.at[2 * z + a2, y], strip_send.at[1], strip_sem.at[4 * (2 * z + a2) + y],
               x=x, zl=0, y=x, zh=2 + b2 // 2, k=lax.rem(b2, 2)),
    ]
    sent[0].start()
    sent[1].start()
    eliminate(work, parts, 1)
    end(groups[1], zh_b)
    for copy in sent[2:]:
        copy.start()
    eliminate(work, parts, 2)
    eliminate(work, parts, 3)
    assemble(work, parts, inverse)

    def arrived(j):
        remote(one, land.at[j], last_send.at[0], land_sem.at[j], k=1 - k).wait_recv()

    def arrived_turned(j):
        remote(one, land_t.at[j], last_send.at[0], land_t_sem.at[j], k=1 - k).wait_recv()

    def arrived_strips(j):
        for s in range(4):
            remote(strip, strips.at[j, s], strip_send.at[0], strip_sem.at[4 * j + s], k=1 - k).wait_recv()
        return jnp.concatenate([strips[j, s] for s in range(4)], axis=0)

    @pl.when(is_diag)
    def _():
        for j in range(4):
            @pl.when(q >= j)
            def _():
                start = pl.multiple_of(128 * (q * (q + 1) // 2 + j), 128)
                out_ref[:, 128 * j:128 * j + 128] = lead_ref[pl.ds(start, 128), :]

            @pl.when(q < j)
            def _():
                start = pl.multiple_of(128 * (j * (j + 1) // 2 + q), 128)
                out_ref[:, 128 * j:128 * j + 128] = lead_ref[pl.ds(start, 128), :].T

    @pl.when(dx == 1)
    def _():
        for j in range(4):
            arrived(j)
            out_ref[:, 128 * j:128 * j + 128] = land[j]

    @pl.when(dx == 3)
    def _():
        for j in range(4):
            arrived(j)
            out_ref[:, 128 * j:128 * j + 128] = land[j].T

    @pl.when(dx == 2)
    def _():
        for j in range(4):
            arrived(j)
            arrived_turned(j)
            out_ref[:, 128 * j:128 * j + 128] = land[j] + land_t[j].T

    @pl.when(strip_direct)
    def _():
        for j in range(4):
            out_ref[:, 128 * j:128 * j + 128] = arrived_strips(j)

    @pl.when(strip_turned)
    def _():
        for j in range(4):
            out_ref[:, 128 * j:128 * j + 128] = arrived_strips(j).T

    @pl.when(leader)
    def _():
        slab = out_ref[...]
        for c in range(8):
            slab_out[c] = dot_rhs_t(slab, inverse[64 * c:64 * c + 64, :])
            if c:
                remote(slab_out.at[c], slab_out.at[0], panel_sem.at[c], panel_sem.at[0], x=c // 2, zl=c % 2).start()
        panel_ref[...] = slab_out[0]
        for c in range(1, 8):
            remote(slab_out.at[c], slab_out.at[0], panel_sem.at[c], panel_sem.at[0], x=c // 2, zl=c % 2).wait_send()

    @pl.when(jnp.logical_not(leader))
    def _():
        remote(slab_out.at[1], slab_out.at[0], panel_sem.at[1], panel_sem.at[0], k=1 - k).wait_recv()
        panel_ref[...] = slab_out[0]

    for copy in sent:
        copy.wait_send()


def whole(blocks, factors, live):
    vmem, hbm = pl.BlockSpec(memory_space=pltpu.VMEM), pl.BlockSpec(memory_space=pl.ANY)
    f32, bf16 = jnp.float32, jnp.bfloat16
    dma = pltpu.SemaphoreType.DMA

    def buffers(n):
        return [
            pltpu.VMEM((4, 4, n, 128), f32),
            pltpu.VMEM((4, 4, n, 128), bf16),
            pltpu.VMEM((4, 4, n, 128), bf16),
            pltpu.VMEM((4, 4, n, 128), bf16),
            pltpu.VMEM((3, 4, n, 128), bf16),
            pltpu.VMEM((4, n, 128), f32),
            pltpu.VMEM((4, n, 128), bf16),
            pltpu.VMEM((3, n, 128), bf16),
        ]

    return pl.pallas_call(
        whole_kernel,
        out_shape=(jax.ShapeDtypeStruct((128, 512), f32), jax.ShapeDtypeStruct((128, 64), f32)),
        in_specs=[pl.BlockSpec(memory_space=pltpu.SMEM), hbm, hbm],
        out_specs=(vmem, vmem),
        scratch_shapes=[
            pltpu.VMEM((4, 512, 512), f32),
            pltpu.VMEM((2048, 512), bf16),
            dma((2,)),
            pltpu.VMEM((16, 16, 128), f32),
            pltpu.VMEM((16, 16, 16, 128), f32),
            pltpu.VMEM((16, 16, 128), f32),
            pltpu.VMEM((WAYS, 256, 256), f32),
            pltpu.VMEM((8, 256, 256), f32),
            pltpu.VMEM((4, 512, 512), bf16),
            pltpu.VMEM((4, 512, 512), bf16),
            pltpu.VMEM((4, 512, 512), bf16),
            pltpu.VMEM((4, 512, 512), bf16),
            pltpu.VMEM((2, 512, 512), bf16),
            pltpu.VMEM((2, 512, 512), bf16),
            pltpu.VMEM((2048, 1024), bf16),
            pltpu.VMEM((512, 512), bf16),
            pltpu.VMEM((1024, 512), bf16),
            pltpu.VMEM((2, 4, 256, 256), f32),
            pltpu.VMEM((2, 2, 128, 256), f32),
            pltpu.VMEM((1280, 128), f32),
            pltpu.VMEM((640, 128), f32),
            pltpu.VMEM((640, 128), f32),
            pltpu.VMEM((3, 160, 128), f32),
            pltpu.VMEM((160, 128), f32),
            pltpu.VMEM((3, 40, 128), f32),
            pltpu.VMEM((1280, 128), f32),
            pltpu.VMEM((512, 512), f32),
            pltpu.VMEM((4, 128, 128), f32),
            pltpu.VMEM((512, 512), f32),
            *buffers(128),
            *buffers(160),
            pltpu.VMEM((128, 128), f32),
            pltpu.VMEM((160, 128), f32),
            pltpu.VMEM((4, 128, 128), f32),
            pltpu.VMEM((4, 128, 128), f32),
            pltpu.VMEM((4, 4, 32, 128), f32),
            pltpu.VMEM((8, 128, 64), f32),
            dma((14,)), dma((14,)), dma((4,)), dma((4,)), dma((4,)), dma((16,)), dma((2,)), dma((8,)),
            dma((12,)), dma((12,)), dma((14,)), dma((14,)),
        ],
        compiler_params=pltpu.CompilerParams(
            vmem_limit_bytes=58 << 20, collective_id=0, has_side_effects=True),
        cost_estimate=pl.CostEstimate(flops=20 << 30, bytes_accessed=8 << 20, transcendentals=0),
    )(live, factors, blocks)


def body(blocks, factors, block_live):
    return whole(blocks, factors, block_live)


def solution(mesh):
    split = Mesh(mesh.devices.reshape(4, 4, 2, 4, 2), AXES)
    row, col = ("y", "zh", "k"), ("x", "zl")
    return jax.shard_map(
        body, mesh=split, in_specs=(P(row, col), P(row, None, None), P(row)),
        out_specs=(P(row, col), P(row, col)), check_vma=False)
```

```python
import jax
import jax.numpy as jnp
from jax import lax
from jax.experimental import pallas as pl
from jax.experimental.pallas import tpu as pltpu
from jax.sharding import Mesh
from jax.sharding import PartitionSpec as P

HI = lax.Precision.HIGHEST
STEP = 8
WAYS = 4


def dot_f32(a, b):
    return jnp.dot(a, b, precision=HI, preferred_element_type=jnp.float32)


def dot_bf16(a, b):
    return jnp.dot(a, b, preferred_element_type=jnp.float32)


def dot_lhs_t(a, b):
    return lax.dot_general(a, b, (((0,), (0,)), ((), ())), preferred_element_type=jnp.float32)


def three_parts(v):
    high = v.astype(jnp.bfloat16)
    rest = v - high.astype(jnp.float32)
    mid = rest.astype(jnp.bfloat16)
    return high, mid, (rest - mid.astype(jnp.float32)).astype(jnp.bfloat16)


def whiten_block(high, low, segment):
    top = dot_bf16(high[:256, :256], segment[:256]) + dot_bf16(low[:256, :256], segment[:256])
    bottom = dot_bf16(high[256:], segment) + dot_bf16(low[256:], segment)
    return top.astype(jnp.bfloat16), bottom.astype(jnp.bfloat16)


def packed_at(r, c):
    return pl.ds(128 * (r * (r + 1) // 2 + c), 128)


def factor(work, p):
    sub = lax.broadcasted_iota(jnp.int32, (8, 128), 0)
    lan = lax.broadcasted_iota(jnp.int32, (8, 128), 1)
    base = 128 * p
    a = [work[base + 8 * g:base + 8 * g + 8, base:base + 128] for g in range(16)]
    x = [jnp.where(sub + 8 * g == lan, 1.0, 0.0) for g in range(16)]
    scale = []
    for k in range(0, 128, STEP):
        g0, s0 = k // 8, k % 8
        arow = [a[g0][s0 + j:s0 + j + 1, :] for j in range(STEP)]
        xrow = [x[g0][s0 + j:s0 + j + 1, :] for j in range(STEP)]
        cols = {g: [jnp.broadcast_to(a[g][:, k + j:k + j + 1], (8, 128)) for j in range(STEP)] for g in range(g0, 16)}
        entry = [[cols[g0][j][s0 + i:s0 + i + 1, :] for j in range(STEP)] for i in range(STEP)]
        ratio = [[None] * STEP for _ in range(STEP)]
        inv = []
        for j in range(STEP):
            inv.append(1.0 / entry[j][j])
            scale.append(entry[j][j])
            for i in range(j + 1, STEP):
                t = entry[i][j] * inv[j]
                ratio[i][j] = t
                for m in range(j + 1, i + 1):
                    entry[i][m] = entry[i][m] - t * entry[m][j]
                arow[i] = arow[i] - t * arow[j]
                xrow[i] = xrow[i] - t * xrow[j]
        arow_n = [arow[j] * inv[j] for j in range(STEP)]
        xrow_n = [xrow[j] * inv[j] for j in range(STEP)]
        for g in range(g0, 16):
            c = cols[g]
            for i in range(1, STEP):
                for j in range(i):
                    c[i] = c[i] - c[j] * ratio[i][j]
            if g == g0:
                c = [jnp.where(sub > s0 + j, c[j], 0.0) for j in range(STEP)]
                if s0 + STEP == 8 and STEP == 1:
                    continue
            for j in range(STEP):
                a[g] = a[g] - c[j] * arow_n[j]
                x[g] = x[g] - c[j] * xrow_n[j]
    whole = jnp.concatenate(x, axis=0)
    return whole * lax.rsqrt(jnp.concatenate(scale, axis=0))


def dot_rhs_t(a, b):
    return lax.dot_general(a, b, (((1,), (1,)), ((), ())), precision=HI, preferred_element_type=jnp.float32)


def eliminate(work, parts, p):
    own = factor(work, p)
    parts[p] = own
    if p < 3:
        base = 128 * p + 128
        panel = dot_rhs_t(work[base:512, base - 128:base], own)
        work[base:512, base - 128:base] = panel
        work[base:512, base:512] = work[base:512, base:512] - dot_rhs_t(panel, panel)


def assemble(work, parts, out_ref):
    zero = jnp.zeros((128, 128), jnp.float32)
    out_ref[0:256, 256:512] = jnp.zeros((256, 256), jnp.float32)
    for h in range(2):
        o = 256 * h
        first, last = parts[2 * h], parts[2 * h + 1]
        out_ref[o:o + 128, o:o + 128] = first
        out_ref[o:o + 128, o + 128:o + 256] = zero
        out_ref[o + 128:o + 256, o + 128:o + 256] = last
        out_ref[o + 128:o + 256, o:o + 128] = -dot_f32(last, dot_f32(work[o + 128:o + 256, o:o + 128], first))
    out_ref[256:512, 0:256] = -dot_f32(
        out_ref[256:512, 256:512], dot_f32(work[256:512, 0:256], out_ref[0:256, 0:256]))


AXES = ("y", "zh", "k", "x", "zl")
MESH = pl.DeviceIdType.MESH


def remote(src, dst, send, recv, **where):
    return pltpu.make_async_remote_copy(
        src_ref=src, dst_ref=dst, send_sem=send, recv_sem=recv, device_id=where, device_id_type=MESH)


def wrapped(i):
    return lax.rem(i + 8, 4)


def greet(barrier, **where):
    pl.semaphore_signal(barrier, inc=1, device_id=where, device_id_type=MESH)


def row_partners(barrier, y, zh, k):
    greet(barrier, k=1 - k)
    for d in range(1, 4):
        greet(barrier, y=wrapped(y + d))
        greet(barrier, zh=wrapped(zh + d))


def whole_kernel(live_ref, factors_hbm, blocks_hbm, out_ref, panel_ref, factors_ref, blocks_ref, load_sem,
                 packed, spread, small, wide, inverse_of, high_all, low_all,
                 near, nxt, relay, far, pair, side, half, acc, tmp,
                 lead_in, lead_from_k, lead_part_k, lead_from_y, lead_part_y, lead_from_zh, lead_ref,
                 work, parts, inverse,
                 mine_a, away_a, from_k_a, part_k_a, from_y_a, mine_y_a, part_y_a, from_zh_a,
                 mine_b, away_b, from_k_b, part_k_b, from_y_b, mine_y_b, part_y_b, from_zh_b,
                 final_a, final_b, land, land_t, strips, slab_out,
                 send, recv, last_send, land_sem, land_t_sem, strip_sem, strip_send, panel_sem,
                 gather_send, gather_recv, lead_send, lead_recv):
    y, zh, k = lax.axis_index("y"), lax.axis_index("zh"), lax.axis_index("k")
    x, z = lax.axis_index("x"), lax.axis_index("zl")
    f32, bf16 = jnp.float32, jnp.bfloat16
    h = x // 2
    leader = (x == 0) & (z == 0)
    zr, q = zh // 2, 2 * lax.rem(zh, 2) + k
    own_at, near_at = pl.multiple_of(512 * z, 512), pl.multiple_of(512 - 512 * z, 512)
    dx = wrapped(y - x)
    is_direct = (dx == 1) | (dx == 2)
    is_turned = (dx == 3) | (dx == 2)
    strip_direct = (dx == 0) & (zr == 0) & (z == 1)
    strip_turned = (dx == 0) & (zr == 1) & (z == 0)
    is_diag = (dx == 0) & (zr == z)

    loads = [pltpu.make_async_copy(factors_hbm, factors_ref, load_sem.at[0]),
             pltpu.make_async_copy(blocks_hbm, blocks_ref, load_sem.at[1])]
    for copy in loads:
        copy.start()
    barrier = pltpu.get_barrier_semaphore()
    row_partners(barrier, y, zh, k)

    @pl.when(is_direct)
    def _():
        for j in range(4):
            b = 4 * z + j
            greet(barrier, k=1 - lax.rem(q, 2), y=2 * (q // 2) + lax.rem(b, 2), zh=b // 2, x=x, zl=zr)

    @pl.when(is_turned)
    def _():
        for j in range(4):
            greet(barrier, k=1 - j % 2, y=2 * (j // 2) + k, zh=zh, x=y, zl=z)

    @pl.when(strip_direct)
    def _():
        for j in range(4):
            for s in range(4):
                greet(barrier, k=1 - k, y=s, zh=(j + 3) % 4, x=x, zl=zh)

    @pl.when(strip_turned)
    def _():
        for j in range(4):
            for s in range(4):
                greet(barrier, k=1 - j % 2, y=s, zh=lax.rem(2 * (zh - 2) + k + 3, 4), x=x, zl=j // 2)

    greet(barrier, zl=1 - z)
    greet(barrier, x=wrapped(x + 1))
    greet(barrier, x=wrapped(x - 1))

    @pl.when(leader)
    def _():
        pl.semaphore_wait(barrier, 23)

    @pl.when(jnp.logical_not(leader))
    def _():
        greet(barrier, x=0, zl=0)
        pl.semaphore_wait(barrier, 16)

    relayed, nears, nexts = [], [], []
    for f in range(4):
        rows = pl.ds(512 * f, 512)
        if f < 2:
            rows_far = pl.ds(pl.multiple_of(1024 * (1 - h) + 512 * f, 512), 512)
            relayed.append(remote(blocks_hbm.at[rows_far], relay.at[f], gather_send.at[8 + f], gather_recv.at[8 + f], x=wrapped(x + 1)))
            relayed[f].start()
        nears.append(remote(blocks_hbm.at[rows], near.at[f], gather_send.at[f], gather_recv.at[f], zl=1 - z))
        nears[f].start()
        nexts.append(remote(blocks_hbm.at[rows], nxt.at[f], gather_send.at[4 + f], gather_recv.at[4 + f], x=wrapped(x - 1)))
        nexts[f].start()

    def prepare():
        row = lax.broadcasted_iota(jnp.int32, (128, 128), 0)
        lane = lax.broadcasted_iota(jnp.int32, (128, 128), 1)
        same = (row // 16) == (lane // 16)
        for f in range(4):
            for d in range(4):
                tile = factors_ref[f, pl.ds(128 * d, 128), pl.ds(128 * d, 128)]
                tile = jnp.where(same, tile, 0.0)
                total = tile[0:16]
                for b in range(1, 8):
                    total = total + tile[16 * b:16 * b + 16]
                packed[:, 4 * f + d, :] = total
        high, mid, low = three_parts(packed[...].reshape(256, 128))
        for j in range(16):
            pick = jnp.where(same & (row % 16 == j), 1.0, 0.0).astype(jnp.bfloat16)
            spread[j] = (dot_bf16(high, pick) + dot_bf16(mid, pick) + dot_bf16(low, pick)).reshape(16, 16, 128)
        lane16 = lax.broadcasted_iota(jnp.int32, (16, 128), 1) % 16
        rows = []
        for i in range(16):
            value = jnp.where(lane16 == i, 1.0, 0.0)
            for j in range(i):
                value = value - spread[j, i] * rows[j]
            value = value / spread[i, i]
            rows.append(value)
            small[i] = value
        row2 = lax.broadcasted_iota(jnp.int32, (256, 256), 0)
        lane2 = lax.broadcasted_iota(jnp.int32, (256, 256), 1)

        def spread_out(block, slot):
            for d in range(2):
                narrow = small[:, 2 * block + d, :]
                wide[slot, 128 * d:128 * d + 128, 128 * d:128 * d + 128] = jnp.where(
                    same, jnp.concatenate([narrow] * 8, axis=0), 0.0)
                wide[slot, 128 * d:128 * d + 128, 128 - 128 * d:256 - 128 * d] = jnp.zeros((128, 128), jnp.float32)
            return wide[slot]

        def grow(group, _):
            blocks = [WAYS * group + w for w in range(WAYS)]
            at = [pl.ds(pl.multiple_of(256 * (b % 2), 256), 256) for b in blocks]
            held = [spread_out(b, w) for w, b in enumerate(blocks)]
            for s in (16, 32, 64, 128):
                mask = ((row2 // (2 * s)) == (lane2 // (2 * s))) & (row2 % (2 * s) >= s) & (lane2 % (2 * s) < s)
                lower = [slice(2 * s * g + s, 2 * s * g + 2 * s) for g in range(256 // (2 * s))]
                odd = lambda v: jnp.concatenate([v[sl] for sl in lower], axis=0)
                first = [dot_f32(odd(jnp.where(mask, factors_ref[b // 2, at[w], at[w]], 0.0)), held[w]) for w, b in enumerate(blocks)]
                full = []
                for w in range(WAYS):
                    pieces = []
                    for g in range(256 // (2 * s)):
                        pieces.append(jnp.zeros((s, 256), jnp.float32))
                        pieces.append(first[w][g * s:(g + 1) * s])
                    full.append(jnp.concatenate(pieces, axis=0))
                second = [dot_f32(odd(held[w]), full[w]) for w in range(WAYS)]
                for w in range(WAYS):
                    pieces = []
                    for g in range(256 // (2 * s)):
                        pieces.append(held[w][2 * s * g:2 * s * g + s])
                        pieces.append(held[w][2 * s * g + s:2 * s * g + 2 * s] - second[w][g * s:(g + 1) * s])
                    held[w] = jnp.concatenate(pieces, axis=0)
            for w, b in enumerate(blocks):
                inverse_of[b] = held[w]
            return _

        lax.fori_loop(0, 8 // WAYS, grow, 0)

        def finish(f, _):
            live = live_ref[f]
            first, last = inverse_of[2 * f], inverse_of[2 * f + 1]
            corner = -dot_f32(last, dot_f32(factors_ref[f, 256:512, 0:256], first))

            def put(value, r, c):
                index = lax.broadcasted_iota(jnp.int32, (256, 256), 0) + r
                value = jnp.where(index < live, value, 0.0)
                high = value.astype(jnp.bfloat16)
                high_all[f, r:r + 256, c:c + 256] = high
                low_all[f, r:r + 256, c:c + 256] = (value - high.astype(jnp.float32)).astype(jnp.bfloat16)

            put(first, 0, 0)
            put(corner, 256, 0)
            put(last, 256, 256)
            put(jnp.zeros((256, 256), jnp.float32), 0, 256)
            start = pl.multiple_of(512 * f, 512)
            top, bottom = whiten_block(high_all[f], low_all[f], blocks_ref[pl.ds(start, 512), :])
            pair[pl.ds(start, 256), pl.ds(own_at, 512)] = top
            pair[pl.ds(start + 256, 256), pl.ds(own_at, 512)] = bottom
            return _

        lax.fori_loop(0, 4, finish, 0)
        for big, small_col in ((0, 0), (1, 0), (1, 1)):
            tile = dot_lhs_t(pair[:, pl.ds(pl.multiple_of(own_at + 256 * big, 256), 256)], pair[:, pl.ds(pl.multiple_of(own_at + 256 * small_col, 256), 256)])
            for i in range(2):
                for j in range(2):
                    r, c = 2 * big + i, 2 * small_col + j
                    if r >= c:
                        lead_in[packed_at(r, c), :] = tile[128 * i:128 * i + 128, 128 * j:128 * j + 128]

    def place(value, slot, put):
        tmp[slot] = value.reshape(2, 128, 256)
        kept, gone = tmp[slot, 1 - k], tmp[slot, k].astype(bf16)
        for j in range(2):
            put(j, kept[:, 128 * j:128 * j + 128], gone[:, 128 * j:128 * j + 128])

    groups = (
        (0, 128, mine_a, away_a, from_k_a, part_k_a, from_y_a, mine_y_a, part_y_a, from_zh_a, final_a),
        (1, 160, mine_b, away_b, from_k_b, part_k_b, from_y_b, mine_y_b, part_y_b, from_zh_b, final_b),
    )

    def send_k(group):
        g, _, mine, away, from_k = group[:5]
        copy = remote(away, from_k, send.at[7 * g], recv.at[7 * g], k=1 - k)
        copy.start()
        return copy

    def send_y(group, copy):
        g, _, mine, away, from_k, part_k, from_y = group[:7]
        copy.wait()
        for i in range(4):
            total = mine[i] + from_k[i].astype(f32)
            mine[i] = total
            part_k[i] = total.astype(bf16)
        copies = []
        for d in range(1, 4):
            copies.append(remote(part_k.at[wrapped(y + d)], from_y.at[d - 1],
                                 send.at[7 * g + d], recv.at[7 * g + d], y=wrapped(y + d)))
            copies[-1].start()
        return copies

    def send_zh(group, copies):
        g, _, mine, away, from_k, part_k, from_y, mine_y, part_y, from_zh, final = group
        for copy in copies:
            copy.wait()
        total = (mine[y] + from_y[0].astype(f32)) + (from_y[1].astype(f32) + from_y[2].astype(f32))
        mine_y[...] = total
        part_y[...] = total.astype(bf16)
        copies = []
        for d in range(1, 4):
            copies.append(remote(part_y.at[wrapped(zh + d)], from_zh.at[d - 1],
                                 send.at[7 * g + 3 + d], recv.at[7 * g + 3 + d], zh=wrapped(zh + d)))
            copies[-1].start()
        return copies

    def end(group, copies):
        mine_y, part_y, from_zh, final = group[7:]
        for copy in copies:
            copy.wait()
        final[...] = (mine_y[zh] + from_zh[0].astype(f32)) + (from_zh[1].astype(f32) + from_zh[2].astype(f32))

    def forward(f):
        relayed[f].wait()
        copy = remote(relay.at[f], far.at[f], gather_send.at[10 + f], gather_recv.at[10 + f], x=wrapped(x + 1))
        copy.start()
        return copy

    def land_chunk(f):
        nears[f].wait()
        nexts[f].wait()
        high, low = high_all[f], low_all[f]
        top, bottom = whiten_block(high, low, near[f])
        pair[512 * f:512 * f + 256, pl.ds(near_at, 512)] = top
        pair[512 * f + 256:512 * f + 512, pl.ds(near_at, 512)] = bottom
        top, bottom = whiten_block(high, low, nxt[f])
        side[0:256, :] = top
        side[256:512, :] = bottom
        for p in range(2):
            for n in range(4):
                value = dot_lhs_t(side[:, 256 * p:256 * p + 256], pair[512 * f:512 * f + 512, 256 * n:256 * n + 256])
                if f == 0:
                    acc[p, n] = value
                elif f < 3:
                    acc[p, n] += value
                else:
                    def put(j, kept, gone):
                        mine_a[2 * p + j, n, :, :] = kept
                        away_a[2 * p + j, n, :, :] = gone
                    place(acc[p, n] + value, n % 2, put)

    def lead_rows(ki, yi=None, zi=None):
        if yi is None:
            return pl.ds(pl.multiple_of(640 * ki, 8), 640)
        if zi is None:
            return pl.ds(pl.multiple_of(640 * ki + 160 * yi, 8), 160)
        return pl.ds(pl.multiple_of(640 * ki + 160 * yi + 40 * zi, 8), 40)

    def lead_k():
        copy = remote(lead_in.at[lead_rows(1 - k)], lead_from_k, lead_send.at[0], lead_recv.at[0], k=1 - k)
        copy.start()
        return copy

    def lead_y(copy):
        copy.wait()
        lead_part_k[...] = lead_in[lead_rows(k), :] + lead_from_k[...]
        copies = []
        for d in range(1, 4):
            copies.append(remote(lead_part_k.at[lead_rows(0, wrapped(y + d))], lead_from_y.at[d - 1],
                                 lead_send.at[d], lead_recv.at[d], y=wrapped(y + d)))
            copies[-1].start()
        return copies

    def lead_zh(copies):
        for copy in copies:
            copy.wait()
        lead_part_y[...] = lead_part_k[lead_rows(0, y), :] + lead_from_y[0] + lead_from_y[1] + lead_from_y[2]
        copies = []
        for d in range(1, 4):
            copies.append(remote(lead_part_y.at[lead_rows(0, 0, wrapped(zh + d))], lead_from_zh.at[d - 1],
                                 lead_send.at[3 + d], lead_recv.at[3 + d], zh=wrapped(zh + d)))
            copies[-1].start()
        return copies

    def lead_back_zh(copies):
        for copy in copies:
            copy.wait()
        rows = lead_rows(k, y, zh)
        lead_ref[rows, :] = (lead_part_y[lead_rows(0, 0, zh), :] + lead_from_zh[0] + lead_from_zh[1] + lead_from_zh[2])
        copies = []
        for d in range(1, 4):
            copies.append(remote(lead_ref.at[rows], lead_ref.at[rows], lead_send.at[6 + d], lead_recv.at[6 + d], zh=wrapped(zh + d)))
            copies[-1].start()
        return copies

    def lead_back_y(copies):
        for copy in copies:
            copy.wait()
        rows = lead_rows(k, y)
        copies = []
        for d in range(1, 4):
            copies.append(remote(lead_ref.at[rows], lead_ref.at[rows], lead_send.at[9 + d], lead_recv.at[9 + d], y=wrapped(y + d)))
            copies[-1].start()
        return copies

    def lead_back_k(copies):
        for copy in copies:
            copy.wait()
        rows = lead_rows(k)
        copy = remote(lead_ref.at[rows], lead_ref.at[rows], lead_send.at[13], lead_recv.at[13], k=1 - k)
        copy.start()
        return copy

    for copy in loads:
        copy.wait()
    prepare()
    fars = [forward(0)]
    lead_step = lead_k()
    land_chunk(0)
    lead_step = lead_y(lead_step)
    fars.append(forward(1))
    land_chunk(1)
    lead_step = lead_zh(lead_step)
    land_chunk(2)
    land_chunk(3)
    k_a = send_k(groups[0])
    lead_step = lead_back_zh(lead_step)
    for f in range(2):
        fars[f].wait()
        top, bottom = whiten_block(high_all[2 * h + f], low_all[2 * h + f], far[f])
        half[512 * f:512 * f + 256, :] = top
        half[512 * f + 256:512 * f + 512, :] = bottom
    y_a = send_y(groups[0], k_a)
    for p in range(2):
        for n in range(4):
            def put(j, kept, gone):
                mine_b[2 * p + j, n, 0:128, :] = kept
                away_b[2 * p + j, n, 0:128, :] = gone
            place(dot_lhs_t(half[:, 256 * p:256 * p + 256],
                            pair[pl.ds(pl.multiple_of(1024 * h, 1024), 1024), 256 * n:256 * n + 256]), n % 2, put)
    for n in range(2):
        def put(j, kept, gone):
            for s in range(4):
                mine_b[s, (2 * n + j + 3) % 4, 128:160, :] = kept[32 * s:32 * s + 32]
                away_b[s, (2 * n + j + 3) % 4, 128:160, :] = gone[32 * s:32 * s + 32]
        place(dot_lhs_t(pair[:, pl.ds(pl.multiple_of(256 * z, 256), 256)],
                        pair[:, 512 + 256 * n:768 + 256 * n]), n % 2, put)
    k_b = send_k(groups[1])
    lead_step = lead_back_y(lead_step)
    y_b = send_y(groups[1], k_b)
    zh_a = send_zh(groups[0], y_a)
    lead_step = lead_back_k(lead_step)
    lead_step.wait()
    for r in range(4):
        for c in range(r + 1):
            work[128 * r:128 * r + 128, 128 * c:128 * c + 128] = lead_ref[packed_at(r, c), :]
            if r != c:
                work[128 * c:128 * c + 128, 128 * r:128 * r + 128] = jnp.zeros((128, 128), f32)
    eliminate(work, parts, 0)
    zh_b = send_zh(groups[1], y_b)
    end(groups[0], zh_a)

    a, b = 2 * (y // 2) + 1 - k, 2 * zh + lax.rem(y, 2)
    a2, b2 = 1 - k, wrapped(zh + 1)
    one, two, strip = final_a, final_b.at[pl.ds(0, 128)], final_b.at[pl.ds(128, 32)]
    sent = [
        remote(one, land.at[lax.rem(b, 4)], last_send.at[0], land_sem.at[lax.rem(b, 4)],
               x=x, zl=b // 4, y=wrapped(x + 1), zh=2 * z + a // 2, k=lax.rem(a, 2)),
        remote(one, land.at[a], last_send.at[1], land_sem.at[a],
               x=wrapped(x + 1), zl=z, y=x, zh=b // 2, k=lax.rem(b, 2)),
        remote(two, land.at[lax.rem(b, 4)], last_send.at[2], land_sem.at[lax.rem(b, 4)],
               x=x, zl=b // 4, y=wrapped(x + 2), zh=2 * z + a // 2, k=lax.rem(a, 2)),
        remote(two, land_t.at[a], last_send.at[3], land_t_sem.at[a],
               x=wrapped(x + 2), zl=z, y=x, zh=b // 2, k=lax.rem(b, 2)),
        remote(strip, strips.at[b2, y], strip_send.at[0], strip_sem.at[4 * b2 + y],
               x=x, zl=1, y=x, zh=z, k=a2),
        remote(strip, strips.at[2 * z + a2, y], strip_send.at[1], strip_sem.at[4 * (2 * z + a2) + y],
               x=x, zl=0, y=x, zh=2 + b2 // 2, k=lax.rem(b2, 2)),
    ]
    sent[0].start()
    sent[1].start()
    eliminate(work, parts, 1)
    end(groups[1], zh_b)
    for copy in sent[2:]:
        copy.start()
    eliminate(work, parts, 2)
    eliminate(work, parts, 3)
    assemble(work, parts, inverse)

    def arrived(j):
        remote(one, land.at[j], last_send.at[0], land_sem.at[j], k=1 - k).wait_recv()

    def arrived_turned(j):
        remote(one, land_t.at[j], last_send.at[0], land_t_sem.at[j], k=1 - k).wait_recv()

    def arrived_strips(j):
        for s in range(4):
            remote(strip, strips.at[j, s], strip_send.at[0], strip_sem.at[4 * j + s], k=1 - k).wait_recv()
        return jnp.concatenate([strips[j, s] for s in range(4)], axis=0)

    @pl.when(is_diag)
    def _():
        for j in range(4):
            @pl.when(q >= j)
            def _():
                start = pl.multiple_of(128 * (q * (q + 1) // 2 + j), 128)
                out_ref[:, 128 * j:128 * j + 128] = lead_ref[pl.ds(start, 128), :]

            @pl.when(q < j)
            def _():
                start = pl.multiple_of(128 * (j * (j + 1) // 2 + q), 128)
                out_ref[:, 128 * j:128 * j + 128] = lead_ref[pl.ds(start, 128), :].T

    @pl.when(dx == 1)
    def _():
        for j in range(4):
            arrived(j)
            out_ref[:, 128 * j:128 * j + 128] = land[j]

    @pl.when(dx == 3)
    def _():
        for j in range(4):
            arrived(j)
            out_ref[:, 128 * j:128 * j + 128] = land[j].T

    @pl.when(dx == 2)
    def _():
        for j in range(4):
            arrived(j)
            arrived_turned(j)
            out_ref[:, 128 * j:128 * j + 128] = land[j] + land_t[j].T

    @pl.when(strip_direct)
    def _():
        for j in range(4):
            out_ref[:, 128 * j:128 * j + 128] = arrived_strips(j)

    @pl.when(strip_turned)
    def _():
        for j in range(4):
            out_ref[:, 128 * j:128 * j + 128] = arrived_strips(j).T

    @pl.when(leader)
    def _():
        slab = out_ref[...]
        for g in (3, 2, 1, 0):
            depth = 128 * (g + 1)
            both = dot_rhs_t(inverse[128 * g:128 * g + 128, 0:depth], slab[:, 0:depth])
            for c in (2 * g, 2 * g + 1):
                slab_out[c] = both[64 * (c % 2):64 * (c % 2) + 64, :]
                if c:
                    remote(slab_out.at[c], slab_out.at[0], panel_sem.at[c], panel_sem.at[0], x=c // 2, zl=c % 2).start()
        panel_ref[...] = slab_out[0]
        for c in range(1, 8):
            remote(slab_out.at[c], slab_out.at[0], panel_sem.at[c], panel_sem.at[0], x=c // 2, zl=c % 2).wait_send()

    @pl.when(jnp.logical_not(leader))
    def _():
        remote(slab_out.at[1], slab_out.at[0], panel_sem.at[1], panel_sem.at[0], k=1 - k).wait_recv()
        panel_ref[...] = slab_out[0]

    for copy in sent:
        copy.wait_send()


def whole(blocks, factors, live):
    vmem, hbm = pl.BlockSpec(memory_space=pltpu.VMEM), pl.BlockSpec(memory_space=pl.ANY)
    f32, bf16 = jnp.float32, jnp.bfloat16
    dma = pltpu.SemaphoreType.DMA

    def buffers(n):
        return [
            pltpu.VMEM((4, 4, n, 128), f32),
            pltpu.VMEM((4, 4, n, 128), bf16),
            pltpu.VMEM((4, 4, n, 128), bf16),
            pltpu.VMEM((4, 4, n, 128), bf16),
            pltpu.VMEM((3, 4, n, 128), bf16),
            pltpu.VMEM((4, n, 128), f32),
            pltpu.VMEM((4, n, 128), bf16),
            pltpu.VMEM((3, n, 128), bf16),
        ]

    return pl.pallas_call(
        whole_kernel,
        out_shape=(jax.ShapeDtypeStruct((128, 512), f32), jax.ShapeDtypeStruct((64, 128), f32)),
        in_specs=[pl.BlockSpec(memory_space=pltpu.SMEM), hbm, hbm],
        out_specs=(vmem, vmem),
        scratch_shapes=[
            pltpu.VMEM((4, 512, 512), f32),
            pltpu.VMEM((2048, 512), bf16),
            dma((2,)),
            pltpu.VMEM((16, 16, 128), f32),
            pltpu.VMEM((16, 16, 16, 128), f32),
            pltpu.VMEM((16, 16, 128), f32),
            pltpu.VMEM((WAYS, 256, 256), f32),
            pltpu.VMEM((8, 256, 256), f32),
            pltpu.VMEM((4, 512, 512), bf16),
            pltpu.VMEM((4, 512, 512), bf16),
            pltpu.VMEM((4, 512, 512), bf16),
            pltpu.VMEM((4, 512, 512), bf16),
            pltpu.VMEM((2, 512, 512), bf16),
            pltpu.VMEM((2, 512, 512), bf16),
            pltpu.VMEM((2048, 1024), bf16),
            pltpu.VMEM((512, 512), bf16),
            pltpu.VMEM((1024, 512), bf16),
            pltpu.VMEM((2, 4, 256, 256), f32),
            pltpu.VMEM((2, 2, 128, 256), f32),
            pltpu.VMEM((1280, 128), f32),
            pltpu.VMEM((640, 128), f32),
            pltpu.VMEM((640, 128), f32),
            pltpu.VMEM((3, 160, 128), f32),
            pltpu.VMEM((160, 128), f32),
            pltpu.VMEM((3, 40, 128), f32),
            pltpu.VMEM((1280, 128), f32),
            pltpu.VMEM((512, 512), f32),
            pltpu.VMEM((4, 128, 128), f32),
            pltpu.VMEM((512, 512), f32),
            *buffers(128),
            *buffers(160),
            pltpu.VMEM((128, 128), f32),
            pltpu.VMEM((160, 128), f32),
            pltpu.VMEM((4, 128, 128), f32),
            pltpu.VMEM((4, 128, 128), f32),
            pltpu.VMEM((4, 4, 32, 128), f32),
            pltpu.VMEM((8, 64, 128), f32),
            dma((14,)), dma((14,)), dma((4,)), dma((4,)), dma((4,)), dma((16,)), dma((2,)), dma((8,)),
            dma((12,)), dma((12,)), dma((14,)), dma((14,)),
        ],
        compiler_params=pltpu.CompilerParams(
            vmem_limit_bytes=58 << 20, collective_id=0, has_side_effects=True),
        cost_estimate=pl.CostEstimate(flops=20 << 30, bytes_accessed=8 << 20, transcendentals=0),
    )(live, factors, blocks)


def body(blocks, factors, block_live):
    slab, panel = whole(blocks, factors, block_live)
    return slab, panel.T


def solution(mesh):
    split = Mesh(mesh.devices.reshape(4, 4, 2, 4, 2), AXES)
    row, col = ("y", "zh", "k"), ("x", "zl")
    return jax.shard_map(
        body, mesh=split, in_specs=(P(row, col), P(row, None, None), P(row)),
        out_specs=(P(row, col), P(row, col)), check_vma=False)
```
